32 devices in a mesh: ctx: 4 (over z), row: 4 (over y, x), col: 2 (over core).
Axes of the slice: x: 2, y: 2, z: 4, core: 2. Of those that a mesh axis runs over, the one named last changes fastest.
Arguments:
- patches: bfloat16 [3072, 2048], P(('ctx', 'row'), 'col'), may hold values from -6 to 6
- visible: int32 [3072], P(('ctx', 'row')), may hold values from -1 to 262143, as said below
- ln_gain: float32 [2048], replicated, may hold values from 0.1 to 1.9
- ln_bias: float32 [2048], replicated, may hold values from -3 to 3
- w_query: bfloat16 [2048, 2048], P('row', 'col')
- w_key: bfloat16 [2048, 2048], P('row', 'col')
- w_value: bfloat16 [2048, 2048], P('row', 'col'), may hold values from -0.125 to 0.125
- w_output: bfloat16 [2048, 2048], P('row', 'col'), may hold values from -0.375 to 0.375
Outputs:
- attn_out: float32 [3072, 2048], P(('ctx', 'row'), 'col')
The draws below stay inside these ranges and needn't reach their ends.
Inputs may be any that keep to these rules, and one draw needn't show every extreme that they name: Slots s * 768 to (s + 1) * 768 - 1 form slab s: first the distinct visible patch numbers of that slab in increasing order, all in s * 65536 to (s + 1) * 65536 - 1, then -1 in every remaining slot. Each slab holds 384 or more visible patches, and some slab is full.
All inputs are finite; a program needn't handle non-finite values.
Results may differ from the reference program's by a relative error of at most 0.0094.
Values may be sent and summed in bfloat16 or wider, within the bound.
A program may use at most 128 MiB of HBM per device.

```python
import math
import jax
import jax.numpy as jnp
from jax import lax

D = 2048
HEADS = 16
HEAD_DIM = 128
GRID = 64
TOK_CTX = 768
TOKENS = 3072
REGION = 65536


def draw_visible(key, part):
    slab_count = TOKENS // TOK_CTX
    full_key, count_key, perm_key = jax.random.split(key, 3)
    full_slab = jax.random.randint(full_key, (), 0, slab_count)
    counts = TOK_CTX - jax.random.randint(count_key, (slab_count,), 0, TOK_CTX // 2 + 1)
    slab_ids = jnp.arange(slab_count, dtype=jnp.int32)
    counts = jnp.where(slab_ids == full_slab, TOK_CTX, counts)

    def one_slab(slab):
        chosen = jax.random.permutation(jax.random.fold_in(perm_key, slab), REGION)[:TOK_CTX]
        return jnp.sort(chosen).astype(jnp.int32) + slab * REGION
    picks = jax.vmap(one_slab)(slab_ids)
    slots = jnp.arange(TOK_CTX, dtype=jnp.int32)
    result = jnp.where(slots[None, :] < counts[:, None], picks, -1)
    return result.reshape(TOKENS).astype(jnp.int32)


def shared_base(key):
    return jax.random.normal(jax.random.fold_in(key, 7), (D, D), jnp.float32) / math.sqrt(D)


def draw_w_query(key, part):
    base = shared_base(key)
    return (2.0 * base).astype(jnp.bfloat16)


def draw_w_key(key, part):
    other = jax.random.normal(jax.random.fold_in(key, 11), (D, D), jnp.float32) / math.sqrt(D)
    return other.astype(jnp.bfloat16)


def levels(stream_key, extent, cuts, low, largest):
    def one(axis_at, blocks):
        heights = jax.random.uniform(jax.random.fold_in(jax.random.fold_in(stream_key, 6), axis_at), (blocks,), jnp.float32, low / len(cuts), largest / len(cuts))
        return jnp.repeat(jnp.exp(heights), extent[axis_at] // blocks).reshape((-1,) + (1,) * (len(extent) - axis_at - 1))

    gain = one(*cuts[0])
    for cut in cuts[1:]:
        gain = gain * one(*cut)
    return gain


def noise(key, extent, width, limit, shards=(), kind=jnp.bfloat16):
    entries = jax.random.normal(key, extent, jnp.float32) * width
    if len(shards) > 0:
        entries = levels(key, extent, shards, -0.22, 0.18) * entries
    return jnp.clip(entries, min=-limit, max=limit).astype(kind)


def setup_inputs(seed: int = 0) -> dict:
    streams_of = jax.random.split(jax.random.key(seed), 9)
    patches = noise(streams_of[0], (TOKENS, D), 1.0, 6.0, ((0, 16), (1, 2)))
    visible = draw_visible(jax.random.fold_in(streams_of[8], 71), 0)
    ln_gain = jnp.clip(1.0 + 0.18 * jax.random.normal(streams_of[2], (D,), jnp.float32), 0.1, 1.9)
    ln_bias = noise(streams_of[3], (D,), 0.5, 3.0, (), jnp.float32)
    w_query = draw_w_query(jax.random.fold_in(streams_of[8], 71), 0)
    w_key = draw_w_key(jax.random.fold_in(streams_of[8], 71), 0)
    w_value = noise(streams_of[6], (D, D), D ** -0.5, 0.125, ((0, 4), (1, 2)))
    w_output = noise(streams_of[7], (D, D), (D // 8) ** -0.5, 0.375, ((0, 4), (1, 2)))
    return dict(patches=patches, visible=visible, ln_gain=ln_gain, ln_bias=ln_bias, w_query=w_query, w_key=w_key, w_value=w_value, w_output=w_output)


def embed(visible, full_width):
    patch_id = jnp.maximum(visible, 0)
    plane_size = GRID * GRID
    coord_x = (patch_id // plane_size).astype(jnp.float32)
    coord_y = (patch_id // GRID % GRID).astype(jnp.float32)
    coord_z = (patch_id % GRID).astype(jnp.float32)
    channel = jnp.arange(full_width, dtype=jnp.int32)
    axis_pick = channel % 3
    frequency = jnp.exp(-math.log(10000.0) * (channel // 6 * 6).astype(jnp.float32) / full_width)
    offset_phase = 0.5 * math.pi * (channel // 3 % 2).astype(jnp.float32)
    picked = jnp.where(axis_pick[None, :] == 0, coord_x[:, None], jnp.where(axis_pick[None, :] == 1, coord_y[:, None], coord_z[:, None]))
    return jnp.sin(picked * frequency[None, :] + offset_phase[None, :])

def normalize(hidden, ln_gain, ln_bias):
    center = hidden - lax.optimization_barrier(jnp.mean(hidden, axis=1, keepdims=True))
    spread = lax.optimization_barrier(jnp.mean(center * center, axis=1, keepdims=True))
    return (center * lax.rsqrt(spread + 1e-06) * ln_gain[None, :] + ln_bias[None, :]).astype(jnp.bfloat16)

def reference(patches, visible, ln_gain, ln_bias, w_query, w_key, w_value, w_output):
    hidden = patches.astype(jnp.float32) + embed(visible, D)
    normed = normalize(hidden, ln_gain, ln_bias)
    query_f = jnp.dot(normed, w_query, preferred_element_type=jnp.float32)
    query = (query_f * (1.0 / math.sqrt(HEAD_DIM))).astype(jnp.bfloat16)
    keys = jnp.dot(normed, w_key, preferred_element_type=jnp.float32).astype(jnp.bfloat16)
    values = jnp.dot(normed, w_value, preferred_element_type=jnp.float32).astype(jnp.bfloat16)
    live = visible >= 0
    query_h = query.reshape(TOKENS, HEADS, HEAD_DIM).transpose(1, 0, 2)
    keys_h = keys.reshape(TOKENS, HEADS, HEAD_DIM).transpose(1, 0, 2)
    values_h = values.reshape(TOKENS, HEADS, HEAD_DIM).transpose(1, 0, 2)

    def one_head(parts):
        q_part, k_part, v_part = parts
        scores = jnp.dot(q_part, k_part.T, preferred_element_type=jnp.float32)
        scores = jnp.where(live[None, :], scores, -1e+30)
        top_score = lax.optimization_barrier(jnp.max(scores, axis=1, keepdims=True))
        weights = jnp.exp(scores - top_score)
        totals = lax.optimization_barrier(jnp.sum(weights, axis=1, keepdims=True))
        accum = jnp.dot(weights.astype(jnp.bfloat16), v_part, preferred_element_type=jnp.float32)
        return accum / totals
    mixed = lax.map(one_head, (query_h, keys_h, values_h))
    mixed = mixed.transpose(1, 0, 2).reshape(TOKENS, D).astype(jnp.bfloat16)
    return jnp.dot(mixed, w_output, preferred_element_type=jnp.float32)
```

```python
import functools
import math

import jax
import jax.numpy as jnp
from jax import lax
from jax.experimental import pallas as pl
from jax.experimental.pallas import tpu as pltpu
from jax.sharding import PartitionSpec as P

HEAD_DIM = 128
GRID = 64
MESH = pl.DeviceIdType.MESH
DEAD = -1e30


def embed(visible, full_width):
    patch_id = jnp.maximum(visible, 0)
    plane_size = GRID * GRID
    coord_x = (patch_id // plane_size).astype(jnp.float32)
    coord_y = (patch_id // GRID % GRID).astype(jnp.float32)
    coord_z = (patch_id % GRID).astype(jnp.float32)
    channel = jnp.arange(full_width, dtype=jnp.int32)
    axis_pick = channel % 3
    frequency = jnp.exp(-math.log(10000.0) * (channel // 6 * 6).astype(jnp.float32) / full_width)
    offset_phase = 0.5 * math.pi * (channel // 3 % 2).astype(jnp.float32)
    picked = jnp.where(
        axis_pick[None, :] == 0,
        coord_x[:, None],
        jnp.where(axis_pick[None, :] == 1, coord_y[:, None], coord_z[:, None]),
    )
    return jnp.sin(picked * frequency[None, :] + offset_phase[None, :])


def normalize(hidden, ln_gain, ln_bias):
    center = hidden - jnp.mean(hidden, axis=1, keepdims=True)
    spread = jnp.mean(center * center, axis=1, keepdims=True)
    return (center * lax.rsqrt(spread + 1e-06) * ln_gain[None, :] + ln_bias[None, :]).astype(
        jnp.bfloat16
    )


def body(patches, visible, ln_gain, ln_bias, w_query, w_key, w_value, w_output):
    rows_full = lax.all_gather(patches, "col", axis=1, tiled=True)
    local_rows = rows_full.shape[0]
    hidden = rows_full.astype(jnp.float32) + embed(visible, rows_full.shape[1])
    normed = normalize(hidden, ln_gain, ln_bias)
    col_width = w_query.shape[1]
    slab_rows = lax.all_gather(normed, "row", axis=0, tiled=True)
    input_start = lax.axis_index("row") * w_query.shape[0]
    own_inputs = lax.dynamic_slice_in_dim(slab_rows, input_start, w_query.shape[0], 1)
    joined = jnp.concatenate([w_query, w_key, w_value], axis=1)
    summed = lax.psum_scatter(
        jnp.dot(own_inputs, joined, preferred_element_type=jnp.float32),
        "row",
        scatter_dimension=0,
        tiled=True,
    )
    query_f = summed[:, :col_width]
    key_f = summed[:, col_width : 2 * col_width]
    value_f = summed[:, 2 * col_width :]
    head_count = col_width // HEAD_DIM
    query = (
        (query_f * (1.0 / math.sqrt(HEAD_DIM)))
        .astype(jnp.bfloat16)
        .reshape(local_rows, head_count, HEAD_DIM)
    )
    keys = key_f.astype(jnp.bfloat16)
    values = value_f.astype(jnp.bfloat16)
    key_live = (visible >= 0).astype(jnp.bfloat16)
    best = jnp.full((head_count, local_rows), -1e30, jnp.float32)
    key_piece = lax.all_gather(keys, ("ctx", "row"), axis=0, tiled=True)
    value_piece = lax.all_gather(values, ("ctx", "row"), axis=0, tiled=True)
    live_piece = lax.all_gather(key_live, ("ctx", "row"), axis=0, tiled=True)
    count = key_piece.shape[0]
    scores = jnp.einsum(
        "qhd,nhd->hqn",
        query,
        key_piece.reshape(count, head_count, HEAD_DIM),
        preferred_element_type=jnp.float32,
    )
    scores = jnp.where(live_piece[None, None, :] > 0, scores, -1e30)
    new_best = jnp.maximum(best, jnp.max(scores, axis=2))
    weights = jnp.exp(scores - new_best[:, :, None])
    totals = jnp.sum(weights, axis=2)
    accum = jnp.einsum(
        "hqn,nhd->hqd",
        weights.astype(jnp.bfloat16),
        value_piece.reshape(count, head_count, HEAD_DIM),
        preferred_element_type=jnp.float32,
    )
    best, totals, accum = (new_best, totals, accum)
    mixed = (
        (accum / totals[:, :, None])
        .transpose(1, 0, 2)
        .reshape(local_rows, col_width)
        .astype(jnp.bfloat16)
    )
    mixed_full = lax.all_gather(mixed, "col", axis=1, tiled=True)
    return jnp.dot(
        mixed_full,
        lax.all_gather(w_output, "row", axis=0, tiled=True),
        preferred_element_type=jnp.float32,
    )


def mesh_kernel(
    sizes, patches, vis, chan, gain, bias, live, w_query, w_key, w_value, w_output, out,
    pfull, hid, wfull, wo, xs, lives, send, queries, kv, key_bias, scores, probs, mixed, mrec, parts, got,
    p_sem, wo_sem, w_send, w_recv, w_near, w_own, wf_sem, x_sem, l_send, l_recv,
    a_send, a_recv, f_send, f_recv, m_send, m_recv, o_send, o_recv,
):
    Z, R, hd = sizes
    z, r, c = lax.axis_index("ctx"), lax.axis_index("row"), lax.axis_index("col")
    half, full_width = xs.shape[0] // Z, xs.shape[1]
    depth, cw = w_query.shape
    plane = wfull.shape[2]
    other = 1 - c

    def device(zz, rr, cc):
        return {"ctx": zz, "row": rr, "col": cc}

    def push(src, dst, ssem, rsem, dev):
        copy = pltpu.make_async_remote_copy(
            src_ref=src, dst_ref=dst, send_sem=ssem, recv_sem=rsem, device_id=dev, device_id_type=MESH
        )
        copy.start()
        return copy

    def landed(ref, sem):
        pltpu.make_async_copy(ref, ref, sem).wait()

    sibling = device(z, r, other)
    barrier = pltpu.get_barrier_semaphore()
    for oz in range(Z):
        for orow in range(R):
            for oc in range(2):
                if (oz, orow, oc) != (0, 0, 0) and (oc == 0 or oz == 0):
                    pl.semaphore_signal(
                        barrier,
                        inc=1,
                        device_id=device(lax.rem(z + oz, Z), lax.rem(r + orow, R), lax.rem(c + oc, 2)),
                        device_id_type=MESH,
                    )
    pl.semaphore_wait(barrier, Z * R - 1 + R)

    sent = [
        push(
            patches.at[pl.ds(pl.multiple_of(other * half, half), half)],
            pfull.at[c], p_sem.at[0], p_sem.at[1], sibling,
        )
    ]
    weights = (w_key, w_value, w_query)
    owner = (z * plane) // cw
    col0 = pl.multiple_of(lax.rem(z * plane, cw), plane)
    sub = depth // 2

    def weight_copies(i):
        src = weights[i]
        copies = []
        for o in range(1, R):
            for cc in range(2):
                copies.append(
                    pltpu.make_async_remote_copy(
                        src_ref=src.at[pl.ds(cc * sub, sub), pl.ds(col0, plane)],
                        dst_ref=wfull.at[i, pl.ds(pl.multiple_of(r * depth + cc * sub, sub), sub)],
                        send_sem=w_send.at[i, o, cc],
                        recv_sem=w_recv.at[i, o],
                        device_id=device(z, lax.rem(r + o, R), cc),
                        device_id_type=MESH,
                    )
                )
        own = wfull.at[i, pl.ds(pl.multiple_of(r * depth, depth), depth)]
        copies.append(
            pltpu.make_async_remote_copy(
                src_ref=src.at[:, pl.ds(col0, plane)], dst_ref=own,
                send_sem=w_send.at[i, 0, 0], recv_sem=w_near.at[i],
                device_id=sibling, device_id_type=MESH,
            )
        )
        return copies, pltpu.make_async_copy(src.at[:, pl.ds(col0, plane)], own, w_own.at[i])

    @pl.when(c == owner)
    def _():
        for i in range(3):
            copies, local = weight_copies(i)
            for copy in copies:
                copy.start()
            local.start()

    wo_copy = pltpu.make_async_copy(w_output, wo.at[c], wo_sem.at[2])
    wo_copy.start()
    sent.append(push(w_output, wo.at[c], wo_sem.at[0], wo_sem.at[1], sibling))
    me = z * R + r
    for oz in range(Z):
        for orow in range(R):
            if (oz, orow) != (0, 0):
                sent.append(
                    push(
                        live, lives.at[me], l_send.at[oz * R + orow], l_recv.at[oz * R + orow],
                        device(lax.rem(z + oz, Z), lax.rem(r + orow, R), c),
                    )
                )
    lives[me] = live[...]

    row0 = pl.multiple_of(c * half, half)
    pfull[c] = patches[pl.ds(row0, half), :]

    def embed_rows(t, carry):
        at = pl.multiple_of(t * 8, 8)
        patch_id = jnp.maximum(vis[pl.ds(row0 + at, 8), :], 0)
        coord_x = (patch_id >> 12).astype(jnp.float32)
        coord_y = ((patch_id >> 6) & (GRID - 1)).astype(jnp.float32)
        coord_z = (patch_id & (GRID - 1)).astype(jnp.float32)
        pick = chan[2:3, :]
        coord = jnp.where(pick == 0.0, coord_x, jnp.where(pick == 1.0, coord_y, coord_z))
        hid[pl.ds(at, 8), :] = jnp.sin(coord * chan[0:1, :] + chan[1:2, :])
        return carry

    lax.fori_loop(0, half // 8, embed_rows, 0)
    landed(pfull.at[other], p_sem.at[1])
    own_slab = pl.multiple_of(z * half, half)

    def norm_rows(t, carry):
        at = pl.multiple_of(t * 16, 16)
        rows = pl.ds(at, 16)
        embedded = jnp.concatenate([pfull[0, rows, :], pfull[1, rows, :]], axis=1)
        hidden = embedded.astype(jnp.float32) + hid[rows, :]
        center = hidden - jnp.mean(hidden, axis=1, keepdims=True)
        spread = jnp.mean(center * center, axis=1, keepdims=True)
        normed = center * lax.rsqrt(spread + 1e-06) * gain[...] + bias[...]
        xs[pl.ds(own_slab + at, 16), :] = normed.astype(jnp.bfloat16)
        return carry

    lax.fori_loop(0, half // 16, norm_rows, 0)
    for oz in range(1, Z):
        slab = xs.at[pl.ds(own_slab, half)]
        sent.append(push(slab, slab, x_sem.at[0, oz], x_sem.at[1, oz], device(lax.rem(z + oz, Z), r, c)))

    for oz in range(Z):
        for orow in range(R):
            if (oz, orow) != (0, 0):
                src = lax.rem(z + Z - oz, Z) * R + lax.rem(r + R - orow, R)
                landed(lives.at[src], l_recv.at[oz * R + orow])
    columns = lives[...].reshape(Z * R * 8, 128).T
    for zz in range(Z):
        for rr in range(R):
            for cc in range(2):
                at = (zz * R + rr) * 8 + cc
                key_bias[cc, rr, zz * half : (zz + 1) * half, :] = columns[:half, at : at + 1]

    for i in range(3):
        for o in range(1, R):
            src_row = lax.rem(r + R - o, R)
            block = wfull.at[i, pl.ds(pl.multiple_of(src_row * depth + c * sub, sub), sub)]
            landed(block, w_recv.at[i, o])
            sent.append(push(block, block, wf_sem.at[0, i, o], wf_sem.at[1, i, o], sibling))
    for oz in range(1, Z):
        slab = xs.at[pl.ds(pl.multiple_of(lax.rem(z + Z - oz, Z) * half, half), half)]
        landed(slab, x_sem.at[1, oz])

    scale = 1.0 / math.sqrt(hd)
    for i in range(3):
        mine = wfull.at[i, pl.ds(pl.multiple_of(r * depth, depth), depth)]

        @pl.when(c == owner)
        def _():
            landed(mine, w_own.at[i])

        @pl.when(c != owner)
        def _():
            landed(mine, w_near.at[i])

        for o in range(1, R):
            src_row = lax.rem(r + R - o, R)
            block = wfull.at[i, pl.ds(pl.multiple_of(src_row * depth + other * sub, sub), sub)]
            landed(block, wf_sem.at[1, i, o])
        for j in range(0, R, 2):
            pair = jnp.dot(
                xs[...], wfull[i, :, j * hd : (j + 2) * hd], preferred_element_type=jnp.float32
            )
            if i == 2:
                pair = pair * scale
            pair = pair.astype(jnp.bfloat16)
            send[i, j] = pair[:, :hd]
            send[i, j + 1] = pair[:, hd:]
        for o in range(1, R):
            j = lax.rem(r + o, R)
            dst = queries.at[r] if i == 2 else kv.at[i, c, r]
            sent.append(push(send.at[i, j], dst, a_send.at[i, o], a_recv.at[i, o], device(z, j, c)))
        if i == 2:
            queries[r] = send[i, r]
        else:
            kv[i, c, r] = send[i, r]
            sent.append(push(send.at[i, r], kv.at[i, c, r], f_send.at[i, 0], f_recv.at[i, 0], sibling))
    for i in range(2):
        for o in range(1, R):
            block = kv.at[i, c, lax.rem(r + R - o, R)]
            landed(block, a_recv.at[i, o])
            sent.append(push(block, block, f_send.at[i, o], f_recv.at[i, o], sibling))
    for o in range(1, R):
        landed(queries.at[lax.rem(r + R - o, R)], a_recv.at[2, o])
    for i in range(2):
        for o in range(R):
            landed(kv.at[i, other, lax.rem(r + R - o, R)], f_recv.at[i, o])

    count = xs.shape[0]
    head = z * R + r
    group = head // Z
    lane0 = pl.multiple_of(lax.rem(head, Z) * hd, hd)

    def mixed_copy(block, zz):
        return pltpu.make_async_remote_copy(
            src_ref=mixed.at[block, pl.ds(zz * half, half)],
            dst_ref=mrec.at[block, :, pl.ds(lane0, hd)],
            send_sem=m_send.at[block, zz],
            recv_sem=m_recv.at[lax.rem(head, Z), block],
            device_id=device(zz, group, c),
            device_id_type=MESH,
        )

    def attend(block, carry):
        query = queries[block]
        best = jnp.full((1, count), DEAD, jnp.float32)
        for cc in range(2):
            for rr in range(R):
                score = lax.dot_general(
                    kv[0, cc, rr], query, (((1,), (1,)), ((), ())), preferred_element_type=jnp.float32
                )
                score = score + key_bias[cc, rr]
                scores[cc, rr] = score
                best = jnp.maximum(best, jnp.max(score, axis=0, keepdims=True))
        totals = jnp.zeros((1, count), jnp.float32)
        accum = jnp.zeros((hd, count), jnp.float32)
        for cc in range(2):
            for rr in range(R):
                weight = jnp.exp(scores[cc, rr] - best)
                totals = totals + jnp.sum(weight, axis=0, keepdims=True)
                accum = accum + lax.dot_general(
                    kv[1, cc, rr], weight.astype(jnp.bfloat16), (((0,), (0,)), ((), ())),
                    preferred_element_type=jnp.float32,
                )
        mixed[block] = (accum / totals).T.astype(jnp.bfloat16)
        for zz in range(Z):
            here = jnp.logical_and(z == zz, group == r)

            @pl.when(jnp.logical_not(here))
            def _():
                mixed_copy(block, zz).start()

            @pl.when(here)
            def _():
                mrec[block, :, pl.ds(lane0, hd)] = mixed[block, pl.ds(zz * half, half), :]

        return carry

    lax.fori_loop(0, R, attend, 0)
    for block in range(R):
        for k in range(Z):
            @pl.when(r * Z + k != head)
            def _():
                landed(mrec.at[block, :, pl.ds(k * hd, hd)], m_recv.at[k, block])

    wo_copy.wait()
    landed(wo.at[other], wo_sem.at[1])
    for cc in range(2):
        part = jnp.dot(
            mrec[...].reshape(R * half, depth), wo[cc], preferred_element_type=jnp.float32
        )
        parts[cc] = part.astype(jnp.bfloat16).reshape(R, half, cw)
    for o in range(1, R):
        for oc in range(2):
            j, cc = lax.rem(r + o, R), lax.rem(c + oc, 2)
            sent.append(
                push(parts.at[cc, j], got.at[r, c], o_send.at[o, oc], o_recv.at[o, oc], device(z, j, cc))
            )
    sent.append(push(parts.at[other, r], got.at[r, c], o_send.at[0, 1], o_recv.at[0, 1], sibling))
    got[r, c] = parts[c, r]
    for o in range(R):
        for oc in range(2):
            if (o, oc) != (0, 0):
                landed(got.at[lax.rem(r + R - o, R), lax.rem(c + oc, 2)], o_recv.at[o, oc])
    for cc in range(2):
        total = got[0, cc].astype(jnp.float32)
        for rr in range(1, R):
            total = total + got[rr, cc].astype(jnp.float32)
        out[cc * half : (cc + 1) * half, :] = total

    for copy in sent:
        copy.wait_send()

    @pl.when(c == owner)
    def _():
        for i in range(3):
            for copy in weight_copies(i)[0]:
                copy.wait_send()

    for block in range(R):
        for zz in range(Z):
            @pl.when(jnp.logical_not(jnp.logical_and(z == zz, group == r)))
            def _():
                mixed_copy(block, zz).wait_send()


def fused(sizes, patches, visible, ln_gain, ln_bias, w_query, w_key, w_value, w_output):
    Z, R = sizes
    rows, cw = patches.shape
    depth = w_query.shape[0]
    width = depth * R
    half = rows // 2
    hd = HEAD_DIM
    plane = R * hd
    count = Z * half
    channel = jnp.arange(width, dtype=jnp.int32)
    chan = jnp.stack(
        [
            jnp.exp(-math.log(10000.0) * (channel // 6 * 6).astype(jnp.float32) / width),
            0.5 * math.pi * (channel // 3 % 2).astype(jnp.float32),
            (channel % 3).astype(jnp.float32),
        ]
    )
    live = jnp.where(visible >= 0, 0.0, DEAD).astype(jnp.float32).reshape(2, half)
    live = jnp.pad(live, ((0, 6), (0, 128 - half)))
    vmem = pl.BlockSpec(memory_space=pltpu.VMEM)
    hbm = pl.BlockSpec(memory_space=pl.ANY)
    bf, f32, dma = jnp.bfloat16, jnp.float32, pltpu.SemaphoreType.DMA
    return pl.pallas_call(
        functools.partial(mesh_kernel, (Z, R, hd)),
        out_shape=jax.ShapeDtypeStruct((rows, cw), f32),
        in_specs=[vmem] * 6 + [hbm] * 4,
        out_specs=vmem,
        scratch_shapes=[
            pltpu.VMEM((2, half, cw), bf),
            pltpu.VMEM((half, width), f32),
            pltpu.VMEM((3, width, plane), bf),
            pltpu.VMEM((2, depth, cw), bf),
            pltpu.VMEM((count, width), bf),
            pltpu.VMEM((Z * R, 8, 128), f32),
            pltpu.VMEM((3, R, count, hd), bf),
            pltpu.VMEM((R, count, hd), bf),
            pltpu.VMEM((2, 2, R, count, hd), bf),
            pltpu.VMEM((2, R, count, 1), f32),
            pltpu.VMEM((2, R, count, count), f32),
            pltpu.VMEM((2, R, count, count), bf),
            pltpu.VMEM((R, count, hd), bf),
            pltpu.VMEM((R, half, depth), bf),
            pltpu.VMEM((2, R, half, cw), bf),
            pltpu.VMEM((R, 2, half, cw), bf),
            dma((2,)),
            dma((3,)),
            dma((3, R, 2)),
            dma((3, R)),
            dma((3,)),
            dma((3,)),
            dma((2, 3, R)),
            dma((2, Z)),
            dma((Z * R,)),
            dma((Z * R,)),
            dma((3, R)),
            dma((3, R)),
            dma((2, R)),
            dma((2, R)),
            dma((R, Z)),
            dma((Z, R)),
            dma((R, 2)),
            dma((R, 2)),
        ],
        compiler_params=pltpu.CompilerParams(
            collective_id=0, has_side_effects=True, vmem_limit_bytes=56 * 1024 * 1024
        ),
    )(patches, visible.reshape(rows, 1), chan, ln_gain.reshape(1, width), ln_bias.reshape(1, width),
      live, w_query, w_key, w_value, w_output)


def fits(mesh, patches, w_query):
    Z, R, C = mesh.shape["ctx"], mesh.shape["row"], mesh.shape["col"]
    width = w_query.shape[0]
    half = patches.shape[0] // (Z * R * 2)
    return (
        C == 2
        and Z * R * HEAD_DIM == width
        and (width // C) % (R * HEAD_DIM) == 0
        and width // R == Z * HEAD_DIM
        and half % 16 == 0
        and half <= 128
    )


def solution(mesh):
    placed = (
        P(("ctx", "row"), "col"),
        P(("ctx", "row")),
        P(),
        P(),
        P("row", "col"),
        P("row", "col"),
        P("row", "col"),
        P("row", "col"),
    )

    def run(*args):
        part = body
        if fits(mesh, args[0], args[4]):
            part = functools.partial(fused, (mesh.shape["ctx"], mesh.shape["row"]))
        return jax.shard_map(
            part, mesh=mesh, in_specs=placed, out_specs=P(("ctx", "row"), "col"), check_vma=False
        )(*args)

    return run
```

```python
import functools
import math

import jax
import jax.numpy as jnp
from jax import lax
from jax.experimental import pallas as pl
from jax.experimental.pallas import tpu as pltpu
from jax.sharding import PartitionSpec as P

HEAD_DIM = 128
GRID = 64
MESH = pl.DeviceIdType.MESH
DEAD = -1e30
STEP = 32


def embed(visible, full_width):
    patch_id = jnp.maximum(visible, 0)
    plane_size = GRID * GRID
    coord_x = (patch_id // plane_size).astype(jnp.float32)
    coord_y = (patch_id // GRID % GRID).astype(jnp.float32)
    coord_z = (patch_id % GRID).astype(jnp.float32)
    channel = jnp.arange(full_width, dtype=jnp.int32)
    axis_pick = channel % 3
    frequency = jnp.exp(-math.log(10000.0) * (channel // 6 * 6).astype(jnp.float32) / full_width)
    offset_phase = 0.5 * math.pi * (channel // 3 % 2).astype(jnp.float32)
    picked = jnp.where(
        axis_pick[None, :] == 0,
        coord_x[:, None],
        jnp.where(axis_pick[None, :] == 1, coord_y[:, None], coord_z[:, None]),
    )
    return jnp.sin(picked * frequency[None, :] + offset_phase[None, :])


def normalize(hidden, ln_gain, ln_bias):
    center = hidden - jnp.mean(hidden, axis=1, keepdims=True)
    spread = jnp.mean(center * center, axis=1, keepdims=True)
    return (center * lax.rsqrt(spread + 1e-06) * ln_gain[None, :] + ln_bias[None, :]).astype(
        jnp.bfloat16
    )


def body(patches, visible, ln_gain, ln_bias, w_query, w_key, w_value, w_output):
    rows_full = lax.all_gather(patches, "col", axis=1, tiled=True)
    local_rows = rows_full.shape[0]
    hidden = rows_full.astype(jnp.float32) + embed(visible, rows_full.shape[1])
    normed = normalize(hidden, ln_gain, ln_bias)
    col_width = w_query.shape[1]
    slab_rows = lax.all_gather(normed, "row", axis=0, tiled=True)
    input_start = lax.axis_index("row") * w_query.shape[0]
    own_inputs = lax.dynamic_slice_in_dim(slab_rows, input_start, w_query.shape[0], 1)
    joined = jnp.concatenate([w_query, w_key, w_value], axis=1)
    summed = lax.psum_scatter(
        jnp.dot(own_inputs, joined, preferred_element_type=jnp.float32),
        "row",
        scatter_dimension=0,
        tiled=True,
    )
    query_f = summed[:, :col_width]
    key_f = summed[:, col_width : 2 * col_width]
    value_f = summed[:, 2 * col_width :]
    head_count = col_width // HEAD_DIM
    query = (
        (query_f * (1.0 / math.sqrt(HEAD_DIM)))
        .astype(jnp.bfloat16)
        .reshape(local_rows, head_count, HEAD_DIM)
    )
    keys = key_f.astype(jnp.bfloat16)
    values = value_f.astype(jnp.bfloat16)
    key_live = (visible >= 0).astype(jnp.bfloat16)
    best = jnp.full((head_count, local_rows), -1e30, jnp.float32)
    key_piece = lax.all_gather(keys, ("ctx", "row"), axis=0, tiled=True)
    value_piece = lax.all_gather(values, ("ctx", "row"), axis=0, tiled=True)
    live_piece = lax.all_gather(key_live, ("ctx", "row"), axis=0, tiled=True)
    count = key_piece.shape[0]
    scores = jnp.einsum(
        "qhd,nhd->hqn",
        query,
        key_piece.reshape(count, head_count, HEAD_DIM),
        preferred_element_type=jnp.float32,
    )
    scores = jnp.where(live_piece[None, None, :] > 0, scores, -1e30)
    new_best = jnp.maximum(best, jnp.max(scores, axis=2))
    weights = jnp.exp(scores - new_best[:, :, None])
    totals = jnp.sum(weights, axis=2)
    accum = jnp.einsum(
        "hqn,nhd->hqd",
        weights.astype(jnp.bfloat16),
        value_piece.reshape(count, head_count, HEAD_DIM),
        preferred_element_type=jnp.float32,
    )
    best, totals, accum = (new_best, totals, accum)
    mixed = (
        (accum / totals[:, :, None])
        .transpose(1, 0, 2)
        .reshape(local_rows, col_width)
        .astype(jnp.bfloat16)
    )
    mixed_full = lax.all_gather(mixed, "col", axis=1, tiled=True)
    return jnp.dot(
        mixed_full,
        lax.all_gather(w_output, "row", axis=0, tiled=True),
        preferred_element_type=jnp.float32,
    )


def mesh_kernel(
    sizes, patches, vis, gain, bias, w_query, w_key, w_value, w_output, got,
    ids, id_col, pin, pnear, hid, wfull, wo, xs, send, queries, kv, key_bias, scores, mixed, mrec, parts,
    p_own, z_send, z_recv, near_send, near_recv, wo_sem, w_send, w_recv, w_near, w_own, wf_sem,
    l_send, l_recv, a_send, a_recv, f_send, f_recv, m_send, m_recv, o_send, o_recv, o_own,
):
    Z, R, hd = sizes
    z, r, c = lax.axis_index("ctx"), lax.axis_index("row"), lax.axis_index("col")
    count, full_width = xs.shape
    half = count // Z
    depth, cw = w_query.shape
    plane = wfull.shape[2]
    other = 1 - c
    blocks = half // STEP
    f32, bf16 = jnp.float32, jnp.bfloat16

    def device(zz, rr, cc):
        return {"ctx": zz, "row": rr, "col": cc}

    def remote(src, dst, ssem, rsem, dev):
        return pltpu.make_async_remote_copy(
            src_ref=src, dst_ref=dst, send_sem=ssem, recv_sem=rsem, device_id=dev, device_id_type=MESH
        )

    sent = []

    def push(src, dst, ssem, rsem, dev):
        copy = remote(src, dst, ssem, rsem, dev)
        copy.start()
        sent.append(copy)

    def landed(ref, sem):
        pltpu.make_async_copy(ref, ref, sem).wait()

    sibling = device(z, r, other)
    barrier = pltpu.get_barrier_semaphore()
    for oz in range(Z):
        for orow in range(R):
            for oc in range(2):
                if (oz, orow, oc) != (0, 0, 0) and (oc == 0 or oz == 0):
                    pl.semaphore_signal(
                        barrier,
                        inc=1,
                        device_id=device(lax.rem(z + oz, Z), lax.rem(r + orow, R), lax.rem(c + oc, 2)),
                        device_id_type=MESH,
                    )
    own_patches = pltpu.make_async_copy(patches, pin.at[z], p_own)
    own_patches.start()
    wo_copy = pltpu.make_async_copy(w_output, wo.at[c], wo_sem.at[2])
    wo_copy.start()
    me = z * R + r
    ids[me] = jnp.zeros((8, 128), jnp.int32)
    ids[me, 0:1, 0:half] = vis[:, 0:half]
    ids[me, 1:2, 0:half] = vis[:, half : 2 * half]
    channel = lax.broadcasted_iota(jnp.int32, (1, full_width), 1)
    sixth = channel // 6
    third = channel // 3
    frequency = jnp.exp(-math.log(10000.0) * (sixth * 6).astype(f32) / full_width)
    phase = 0.5 * math.pi * (third % 2).astype(f32)
    pick = channel - third * 3
    pl.semaphore_wait(barrier, Z * R - 1 + R)

    for oz in range(Z):
        for orow in range(R):
            if (oz, orow) != (0, 0):
                push(
                    ids.at[me], ids.at[me], l_send.at[oz * R + orow], l_recv.at[oz * R + orow],
                    device(lax.rem(z + oz, Z), lax.rem(r + orow, R), c),
                )

    def hop(up, far):
        slab = z - far if up else z + far
        block = pin.at[slab]
        src = patches if far == 0 else block
        way = 0 if up else 1
        return remote(
            src, block, z_send.at[way, far], z_recv.at[way, far + 1], device(z + 1 if up else z - 1, r, c)
        )

    def passes(up, far):
        return jnp.logical_and(z >= far, z < Z - 1) if up else jnp.logical_and(z + far < Z, z > 0)

    for up in (True, False):
        @pl.when(passes(up, 0))
        def _():
            hop(up, 0).start()

    weights = (w_key, w_value, w_query)
    owner = (z * plane) // cw
    col0 = pl.multiple_of(lax.rem(z * plane, cw), plane)
    sub = depth // 2

    def weight_copies(i):
        src = weights[i]
        copies = []
        for o in range(1, R):
            for cc in range(2):
                copies.append(
                    remote(
                        src.at[pl.ds(cc * sub, sub), pl.ds(col0, plane)],
                        wfull.at[i, pl.ds(pl.multiple_of(r * depth + cc * sub, sub), sub)],
                        w_send.at[i, o, cc],
                        w_recv.at[i, o],
                        device(z, lax.rem(r + o, R), cc),
                    )
                )
        own = wfull.at[i, pl.ds(pl.multiple_of(r * depth, depth), depth)]
        copies.append(
            remote(src.at[:, pl.ds(col0, plane)], own, w_send.at[i, 0, 0], w_near.at[i], sibling)
        )
        return copies

    def weight_local(i):
        own = wfull.at[i, pl.ds(pl.multiple_of(r * depth, depth), depth)]
        return pltpu.make_async_copy(weights[i].at[:, pl.ds(col0, plane)], own, w_own.at[i])

    @pl.when(c == owner)
    def _():
        for i in range(3):
            for copy in weight_copies(i):
                copy.start()
            weight_local(i).start()

    push(w_output, wo.at[c], wo_sem.at[0], wo_sem.at[1], sibling)
    own_patches.wait()

    def share(slab):
        push(
            pin.at[slab, pl.ds(pl.multiple_of(other * half, half), half)],
            pnear.at[slab], near_send.at[slab], near_recv.at[slab], sibling,
        )

    share(z)

    for oz in range(Z):
        for orow in range(R):
            if (oz, orow) != (0, 0):
                src = lax.rem(z + Z - oz, Z) * R + lax.rem(r + R - orow, R)
                landed(ids.at[src], l_recv.at[oz * R + orow])
    for zz in range(Z):
        columns = ids[zz * R + r].astype(f32).T
        id_col[zz * half : (zz + 1) * half, :] = jnp.where(
            c == 0, columns[:half, 0:1], columns[:half, 1:2]
        )

    def embed_rows(base):
        def run(t, carry):
            at = pl.multiple_of(base + t * 8, 8)
            patch_id = jnp.maximum(id_col[pl.ds(at, 8), :].astype(jnp.int32), 0)
            coord_x = (patch_id >> 12).astype(f32)
            coord_y = ((patch_id >> 6) & (GRID - 1)).astype(f32)
            coord_z = (patch_id & (GRID - 1)).astype(f32)
            coord = jnp.where(pick == 0, coord_x, jnp.where(pick == 1, coord_y, coord_z))
            hid[pl.ds(at, 8), :] = jnp.sin(coord * frequency + phase)
            return carry

        lax.fori_loop(0, half // 8, run, 0)

    row0 = pl.multiple_of(c * half, half)

    def norm_slab(slab):
        landed(pnear.at[slab], near_recv.at[slab])
        base = pl.multiple_of(slab * half, half)

        def run(t, carry):
            at = pl.multiple_of(t * 16, 16)
            mine = pin[slab, pl.ds(row0 + at, 16), :]
            theirs = pnear[slab, pl.ds(at, 16), :]
            left = jnp.where(c == 0, mine, theirs)
            right = jnp.where(c == 0, theirs, mine)
            embedded = jnp.concatenate([left, right], axis=1)
            hidden = embedded.astype(f32) + hid[pl.ds(base + at, 16), :]
            center = hidden - jnp.mean(hidden, axis=1, keepdims=True)
            spread = jnp.mean(center * center, axis=1, keepdims=True)
            normed = center * lax.rsqrt(spread + 1e-06) * gain[...] + bias[...]
            xs[pl.ds(base + at, 16), :] = normed.astype(bf16)
            return carry

        lax.fori_loop(0, half // 16, run, 0)

    embed_rows(0)
    embed_rows(half)
    for far in range(1, Z):
        for up in (True, False):
            slab = z - far if up else z + far

            @pl.when(z >= far if up else z + far < Z)
            def _():
                landed(pin.at[slab], z_recv.at[0 if up else 1, far])

            if far < Z - 1:
                @pl.when(passes(up, far))
                def _():
                    hop(up, far).start()

            @pl.when(z >= far if up else z + far < Z)
            def _():
                remote(
                    pin.at[slab, pl.ds(pl.multiple_of(other * half, half), half)],
                    pnear.at[slab], near_send.at[slab], near_recv.at[slab], sibling,
                ).start()

        if far == 1:
            for zz in range(2, Z):
                embed_rows(zz * half)
            columns = ids[...].astype(f32).reshape(Z * R * 8, 128).T
            dead = jnp.where(columns < 0.0, DEAD, 0.0)
            for zz in range(Z):
                for rr in range(R):
                    for cc in range(2):
                        at = (zz * R + rr) * 8 + cc
                        key_bias[cc, rr, zz * half : (zz + 1) * half, :] = dead[:half, at : at + 1]
            norm_slab(z)
        for up in (True, False):
            slab = z - far if up else z + far

            @pl.when(z >= far if up else z + far < Z)
            def _():
                norm_slab(slab)

    for i in range(3):
        for o in range(1, R):
            src_row = lax.rem(r + R - o, R)
            block = wfull.at[i, pl.ds(pl.multiple_of(src_row * depth + c * sub, sub), sub)]
            landed(block, w_recv.at[i, o])
            push(block, block, wf_sem.at[0, i, o], wf_sem.at[1, i, o], sibling)

    scale = 1.0 / math.sqrt(hd)
    for i in range(3):
        mine = wfull.at[i, pl.ds(pl.multiple_of(r * depth, depth), depth)]

        @pl.when(c == owner)
        def _():
            landed(mine, w_own.at[i])

        @pl.when(c != owner)
        def _():
            landed(mine, w_near.at[i])

        for o in range(1, R):
            src_row = lax.rem(r + R - o, R)
            block = wfull.at[i, pl.ds(pl.multiple_of(src_row * depth + other * sub, sub), sub)]
            landed(block, wf_sem.at[1, i, o])
        for j in range(0, R, 2):
            pair = jnp.dot(
                xs[...], wfull[i, :, j * hd : (j + 2) * hd], preferred_element_type=f32
            )
            if i == 2:
                pair = pair * scale
            pair = pair.astype(bf16)
            if i == 2:
                pair = jnp.concatenate(
                    [
                        pair[zz * half + b * STEP : zz * half + (b + 1) * STEP]
                        for b in range(blocks)
                        for zz in range(Z)
                    ],
                    axis=0,
                )
            send[i, j] = pair[:, :hd]
            send[i, j + 1] = pair[:, hd:]
        for o in range(1, R):
            j = lax.rem(r + o, R)
            dst = queries.at[r] if i == 2 else kv.at[i, c, r]
            push(send.at[i, j], dst, a_send.at[i, o], a_recv.at[i, o], device(z, j, c))
        if i == 2:
            queries[r] = send[i, r]
        else:
            kv[i, c, r] = send[i, r]
            push(send.at[i, r], kv.at[i, c, r], f_send.at[i, 0], f_recv.at[i, 0], sibling)
    for i in range(2):
        for o in range(1, R):
            block = kv.at[i, c, lax.rem(r + R - o, R)]
            landed(block, a_recv.at[i, o])
            push(block, block, f_send.at[i, o], f_recv.at[i, o], sibling)
    for o in range(1, R):
        landed(queries.at[lax.rem(r + R - o, R)], a_recv.at[2, o])
    for i in range(2):
        for o in range(R):
            landed(kv.at[i, other, lax.rem(r + R - o, R)], f_recv.at[i, o])

    head = z * R + r
    group = head // Z
    lane0 = pl.multiple_of(lax.rem(head, Z) * hd, hd)
    chunk = Z * STEP
    wide = R * chunk

    def mixed_copy(b, zz):
        return remote(
            mixed.at[b, :, zz],
            mrec.at[b, :, :, pl.ds(lane0, hd)],
            m_send.at[b, zz],
            m_recv.at[lax.rem(head, Z), b],
            device(zz, group, c),
        )

    def attend(b):
        query = queries[:, b * chunk : (b + 1) * chunk, :].reshape(wide, hd)
        best = jnp.full((1, wide), DEAD, f32)
        for cc in range(2):
            for rr in range(R):
                score = lax.dot_general(
                    kv[0, cc, rr], query, (((1,), (1,)), ((), ())), preferred_element_type=f32
                )
                score = score + key_bias[cc, rr]
                scores[cc, rr] = score
                best = jnp.maximum(best, jnp.max(score, axis=0, keepdims=True))
        totals = jnp.zeros((1, wide), f32)
        accum = jnp.zeros((hd, wide), f32)
        for cc in range(2):
            for rr in range(R):
                weight = jnp.exp(scores[cc, rr] - best)
                totals = totals + jnp.sum(weight, axis=0, keepdims=True)
                accum = accum + lax.dot_general(
                    kv[1, cc, rr], weight.astype(bf16), (((0,), (0,)), ((), ())),
                    preferred_element_type=f32,
                )
        mixed[b] = (accum / totals).T.astype(bf16).reshape(R, Z, STEP, hd)
        for zz in range(Z):
            here = jnp.logical_and(z == zz, group == r)

            @pl.when(jnp.logical_not(here))
            def _():
                mixed_copy(b, zz).start()

            @pl.when(here)
            def _():
                mrec[b, :, :, pl.ds(lane0, hd)] = mixed[b, :, zz]

    def project(b):
        for k in range(Z):
            @pl.when(r * Z + k != head)
            def _():
                landed(mrec.at[b, :, :, pl.ds(k * hd, hd)], m_recv.at[k, b])

        for cc in range(2):
            part = jnp.dot(mrec[b].reshape(R * STEP, depth), wo[cc], preferred_element_type=f32)
            parts[b, cc] = part.astype(bf16).reshape(R, STEP, cw)
        dst = got.at[r, c, pl.ds(b * STEP, STEP)]
        for o in range(1, R):
            for oc in range(2):
                j, cc = lax.rem(r + o, R), lax.rem(c + oc, 2)
                push(parts.at[b, cc, j], dst, o_send.at[b, o, oc], o_recv.at[b, o, oc], device(z, j, cc))
        push(parts.at[b, other, r], dst, o_send.at[b, 0, 1], o_recv.at[b, 0, 1], sibling)
        pltpu.make_async_copy(parts.at[b, c, r], dst, o_own.at[b]).start()

    attend(0)
    wo_copy.wait()
    landed(wo.at[other], wo_sem.at[1])
    for b in range(1, blocks):
        attend(b)
        project(b - 1)
    project(blocks - 1)

    for b in range(blocks):
        rows = pl.ds(b * STEP, STEP)
        landed(got.at[r, c, rows], o_own.at[b])
        for o in range(R):
            for oc in range(2):
                if (o, oc) != (0, 0):
                    src = got.at[lax.rem(r + R - o, R), lax.rem(c + oc, 2), rows]
                    landed(src, o_recv.at[b, o, oc])

    for copy in sent:
        copy.wait_send()
    for far in range(Z - 1):
        for up in (True, False):
            @pl.when(passes(up, far))
            def _():
                hop(up, far).wait_send()

    for far in range(1, Z):
        for up in (True, False):
            slab = z - far if up else z + far

            @pl.when(z >= far if up else z + far < Z)
            def _():
                remote(
                    pin.at[slab, pl.ds(pl.multiple_of(other * half, half), half)],
                    pnear.at[slab], near_send.at[slab], near_recv.at[slab], sibling,
                ).wait_send()

    @pl.when(c == owner)
    def _():
        for i in range(3):
            for copy in weight_copies(i):
                copy.wait_send()

    for b in range(blocks):
        for zz in range(Z):
            @pl.when(jnp.logical_not(jnp.logical_and(z == zz, group == r)))
            def _():
                mixed_copy(b, zz).wait_send()


def fused(sizes, patches, visible, ln_gain, ln_bias, w_query, w_key, w_value, w_output):
    Z, R = sizes
    rows, cw = patches.shape
    depth = w_query.shape[0]
    width = depth * R
    half = rows // 2
    hd = HEAD_DIM
    plane = R * hd
    count = Z * half
    blocks = half // STEP
    vmem = pl.BlockSpec(memory_space=pltpu.VMEM)
    hbm = pl.BlockSpec(memory_space=pl.ANY)
    bf, f32, dma = jnp.bfloat16, jnp.float32, pltpu.SemaphoreType.DMA
    got = pl.pallas_call(
        functools.partial(mesh_kernel, (Z, R, hd)),
        out_shape=jax.ShapeDtypeStruct((R, 2, half, cw), bf),
        in_specs=[hbm] + [vmem] * 3 + [hbm] * 4,
        out_specs=hbm,
        scratch_shapes=[
            pltpu.VMEM((Z * R, 8, 128), jnp.int32),
            pltpu.VMEM((count, 1), f32),
            pltpu.VMEM((Z, rows, cw), bf),
            pltpu.VMEM((Z, half, cw), bf),
            pltpu.VMEM((count, width), f32),
            pltpu.VMEM((3, width, plane), bf),
            pltpu.VMEM((2, depth, cw), bf),
            pltpu.VMEM((count, width), bf),
            pltpu.VMEM((3, R, count, hd), bf),
            pltpu.VMEM((R, count, hd), bf),
            pltpu.VMEM((2, 2, R, count, hd), bf),
            pltpu.VMEM((2, R, count, 1), f32),
            pltpu.VMEM((2, R, count, R * Z * STEP), f32),
            pltpu.VMEM((blocks, R, Z, STEP, hd), bf),
            pltpu.VMEM((blocks, R, STEP, depth), bf),
            pltpu.VMEM((blocks, 2, R, STEP, cw), bf),
            dma,
            dma((2, Z)),
            dma((2, Z)),
            dma((Z,)),
            dma((Z,)),
            dma((3,)),
            dma((3, R, 2)),
            dma((3, R)),
            dma((3,)),
            dma((3,)),
            dma((2, 3, R)),
            dma((Z * R,)),
            dma((Z * R,)),
            dma((3, R)),
            dma((3, R)),
            dma((2, R)),
            dma((2, R)),
            dma((blocks, Z)),
            dma((Z, blocks)),
            dma((blocks, R, 2)),
            dma((blocks, R, 2)),
            dma((blocks,)),
        ],
        compiler_params=pltpu.CompilerParams(
            collective_id=0, has_side_effects=True, vmem_limit_bytes=56 * 1024 * 1024
        ),
    )(patches, visible.reshape(1, rows), ln_gain.reshape(1, width), ln_bias.reshape(1, width),
      w_query, w_key, w_value, w_output)
    return jnp.sum(got.astype(f32), axis=0).reshape(rows, cw)


def fits(mesh, patches, w_query):
    Z, R, C = mesh.shape["ctx"], mesh.shape["row"], mesh.shape["col"]
    width = w_query.shape[0]
    half = patches.shape[0] // (Z * R * 2)
    return (
        C == 2
        and Z * R * HEAD_DIM == width
        and (width // C) % (R * HEAD_DIM) == 0
        and width // R == Z * HEAD_DIM
        and half % STEP == 0
        and half <= 128
    )


def solution(mesh):
    placed = (
        P(("ctx", "row"), "col"),
        P(("ctx", "row")),
        P(),
        P(),
        P("row", "col"),
        P("row", "col"),
        P("row", "col"),
        P("row", "col"),
    )

    def run(*args):
        part = body
        if fits(mesh, args[0], args[4]):
            part = functools.partial(fused, (mesh.shape["ctx"], mesh.shape["row"]))
        return jax.shard_map(
            part, mesh=mesh, in_specs=placed, out_specs=P(("ctx", "row"), "col"), check_vma=False
        )(*args)

    return run
```

```python
import functools
import math

import jax
import jax.numpy as jnp
from jax import lax
from jax.experimental import pallas as pl
from jax.experimental.pallas import tpu as pltpu
from jax.sharding import PartitionSpec as P

HEAD_DIM = 128
GRID = 64
MESH = pl.DeviceIdType.MESH
DEAD = -1e30
STEP = 32
NEAR = (1, 2)


def embed(visible, full_width):
    patch_id = jnp.maximum(visible, 0)
    plane_size = GRID * GRID
    coord_x = (patch_id // plane_size).astype(jnp.float32)
    coord_y = (patch_id // GRID % GRID).astype(jnp.float32)
    coord_z = (patch_id % GRID).astype(jnp.float32)
    channel = jnp.arange(full_width, dtype=jnp.int32)
    axis_pick = channel % 3
    frequency = jnp.exp(-math.log(10000.0) * (channel // 6 * 6).astype(jnp.float32) / full_width)
    offset_phase = 0.5 * math.pi * (channel // 3 % 2).astype(jnp.float32)
    picked = jnp.where(
        axis_pick[None, :] == 0,
        coord_x[:, None],
        jnp.where(axis_pick[None, :] == 1, coord_y[:, None], coord_z[:, None]),
    )
    return jnp.sin(picked * frequency[None, :] + offset_phase[None, :])


def normalize(hidden, ln_gain, ln_bias):
    center = hidden - jnp.mean(hidden, axis=1, keepdims=True)
    spread = jnp.mean(center * center, axis=1, keepdims=True)
    return (center * lax.rsqrt(spread + 1e-06) * ln_gain[None, :] + ln_bias[None, :]).astype(
        jnp.bfloat16
    )


def body(patches, visible, ln_gain, ln_bias, w_query, w_key, w_value, w_output):
    rows_full = lax.all_gather(patches, "col", axis=1, tiled=True)
    local_rows = rows_full.shape[0]
    hidden = rows_full.astype(jnp.float32) + embed(visible, rows_full.shape[1])
    normed = normalize(hidden, ln_gain, ln_bias)
    col_width = w_query.shape[1]
    slab_rows = lax.all_gather(normed, "row", axis=0, tiled=True)
    input_start = lax.axis_index("row") * w_query.shape[0]
    own_inputs = lax.dynamic_slice_in_dim(slab_rows, input_start, w_query.shape[0], 1)
    joined = jnp.concatenate([w_query, w_key, w_value], axis=1)
    summed = lax.psum_scatter(
        jnp.dot(own_inputs, joined, preferred_element_type=jnp.float32),
        "row",
        scatter_dimension=0,
        tiled=True,
    )
    query_f = summed[:, :col_width]
    key_f = summed[:, col_width : 2 * col_width]
    value_f = summed[:, 2 * col_width :]
    head_count = col_width // HEAD_DIM
    query = (
        (query_f * (1.0 / math.sqrt(HEAD_DIM)))
        .astype(jnp.bfloat16)
        .reshape(local_rows, head_count, HEAD_DIM)
    )
    keys = key_f.astype(jnp.bfloat16)
    values = value_f.astype(jnp.bfloat16)
    key_live = (visible >= 0).astype(jnp.bfloat16)
    best = jnp.full((head_count, local_rows), -1e30, jnp.float32)
    key_piece = lax.all_gather(keys, ("ctx", "row"), axis=0, tiled=True)
    value_piece = lax.all_gather(values, ("ctx", "row"), axis=0, tiled=True)
    live_piece = lax.all_gather(key_live, ("ctx", "row"), axis=0, tiled=True)
    count = key_piece.shape[0]
    scores = jnp.einsum(
        "qhd,nhd->hqn",
        query,
        key_piece.reshape(count, head_count, HEAD_DIM),
        preferred_element_type=jnp.float32,
    )
    scores = jnp.where(live_piece[None, None, :] > 0, scores, -1e30)
    new_best = jnp.maximum(best, jnp.max(scores, axis=2))
    weights = jnp.exp(scores - new_best[:, :, None])
    totals = jnp.sum(weights, axis=2)
    accum = jnp.einsum(
        "hqn,nhd->hqd",
        weights.astype(jnp.bfloat16),
        value_piece.reshape(count, head_count, HEAD_DIM),
        preferred_element_type=jnp.float32,
    )
    best, totals, accum = (new_best, totals, accum)
    mixed = (
        (accum / totals[:, :, None])
        .transpose(1, 0, 2)
        .reshape(local_rows, col_width)
        .astype(jnp.bfloat16)
    )
    mixed_full = lax.all_gather(mixed, "col", axis=1, tiled=True)
    return jnp.dot(
        mixed_full,
        lax.all_gather(w_output, "row", axis=0, tiled=True),
        preferred_element_type=jnp.float32,
    )


def sine(x):
    turns = jnp.floor(x * (1.0 / math.pi) + 0.5)
    y = x - turns * 3.140625
    y = y - turns * 9.67502593994140625e-4
    y = y - turns * 1.509957990978376432e-7
    odd = turns - 2.0 * jnp.floor(turns * 0.5)
    y = y * (1.0 - 2.0 * odd)
    y2 = y * y
    tail = y2 * (-1.0 / 39916800.0) + 1.0 / 362880.0
    tail = tail * y2 - 1.0 / 5040.0
    tail = tail * y2 + 1.0 / 120.0
    tail = tail * y2 - 1.0 / 6.0
    return y + y * y2 * tail


def mesh_kernel(
    sizes, patches, vis, gain, bias, w_query, w_key, w_value, w_output, got,
    ids, id_col, pin, pnear, hid, wfull, wo, xs, send, queries, kv, key_bias, scores, mixed, mrec, parts,
    p_own, z_send, z_recv, near_send, near_recv, wo_sem, w_send, w_recv, w_near, w_own, wf_sem, d_send, d_recv,
    l_send, l_recv, a_send, a_recv, f_send, f_recv, m_send, m_recv, o_send, o_recv, o_own,
):
    Z, R, hd = sizes
    z, r, c = lax.axis_index("ctx"), lax.axis_index("row"), lax.axis_index("col")
    count, full_width = xs.shape
    half = count // Z
    depth, cw = w_query.shape
    plane = wfull.shape[2]
    other = 1 - c
    blocks = half // STEP
    f32, bf16 = jnp.float32, jnp.bfloat16

    def device(zz, rr, cc):
        return {"ctx": zz, "row": rr, "col": cc}

    def remote(src, dst, ssem, rsem, dev):
        return pltpu.make_async_remote_copy(
            src_ref=src, dst_ref=dst, send_sem=ssem, recv_sem=rsem, device_id=dev, device_id_type=MESH
        )

    sent = []

    def push(src, dst, ssem, rsem, dev):
        copy = remote(src, dst, ssem, rsem, dev)
        copy.start()
        sent.append(copy)

    def landed(ref, sem):
        pltpu.make_async_copy(ref, ref, sem).wait()

    sibling = device(z, r, other)
    barrier = pltpu.get_barrier_semaphore()
    for oz in range(Z):
        for orow in range(R):
            for oc in range(2):
                if (oz, orow, oc) != (0, 0, 0) and (oc == 0 or oz == 0):
                    pl.semaphore_signal(
                        barrier,
                        inc=1,
                        device_id=device(lax.rem(z + oz, Z), lax.rem(r + orow, R), lax.rem(c + oc, 2)),
                        device_id_type=MESH,
                    )
    own_patches = pltpu.make_async_copy(patches, pin.at[z], p_own)
    own_patches.start()
    wo_copy = pltpu.make_async_copy(w_output, wo.at[c], wo_sem.at[2])
    wo_copy.start()
    me = z * R + r
    ids[me] = jnp.zeros((8, 128), jnp.int32)
    ids[me, 0:1, 0:half] = vis[:, 0:half]
    ids[me, 1:2, 0:half] = vis[:, half : 2 * half]
    channel = lax.broadcasted_iota(jnp.int32, (1, full_width), 1)
    sixth = channel // 6
    third = channel // 3
    frequency = jnp.exp(-math.log(10000.0) * (sixth * 6).astype(f32) / full_width)
    phase = 0.5 * math.pi * (third % 2).astype(f32)
    pick = channel - third * 3
    pl.semaphore_wait(barrier, Z * R - 1 + R)

    for oz in range(Z):
        for orow in range(R):
            if (oz, orow) != (0, 0):
                push(
                    ids.at[me], ids.at[me], l_send.at[oz * R + orow], l_recv.at[oz * R + orow],
                    device(lax.rem(z + oz, Z), lax.rem(r + orow, R), c),
                )

    def hop(up, far):
        slab = z - far if up else z + far
        block = pin.at[slab]
        src = patches if far == 0 else block
        way = 0 if up else 1
        return remote(
            src, block, z_send.at[way, far], z_recv.at[way, far + 1], device(z + 1 if up else z - 1, r, c)
        )

    def passes(up, far):
        return jnp.logical_and(z >= far, z < Z - 1) if up else jnp.logical_and(z + far < Z, z > 0)

    for up in (True, False):
        @pl.when(passes(up, 0))
        def _():
            hop(up, 0).start()

    weights = (w_query, w_key, w_value)
    owner = (z * plane) // cw
    col0 = pl.multiple_of(lax.rem(z * plane, cw), plane)
    sub = depth // 2

    def weight_copies(i):
        src = weights[i]
        copies = []
        for o in NEAR:
            for cc in range(2):
                copies.append(
                    remote(
                        src.at[pl.ds(cc * sub, sub), pl.ds(col0, plane)],
                        wfull.at[i, pl.ds(pl.multiple_of(r * depth + cc * sub, sub), sub)],
                        w_send.at[i, o, cc],
                        w_recv.at[i, o],
                        device(z, r ^ o, cc),
                    )
                )
        own = wfull.at[i, pl.ds(pl.multiple_of(r * depth, depth), depth)]
        copies.append(
            remote(src.at[:, pl.ds(col0, plane)], own, w_send.at[i, 0, 0], w_near.at[i], sibling)
        )
        return copies

    def weight_local(i):
        own = wfull.at[i, pl.ds(pl.multiple_of(r * depth, depth), depth)]
        return pltpu.make_async_copy(weights[i].at[:, pl.ds(col0, plane)], own, w_own.at[i])

    @pl.when(c == owner)
    def _():
        for i in range(3):
            for copy in weight_copies(i):
                copy.start()
            weight_local(i).start()

    push(w_output, wo.at[c], wo_sem.at[0], wo_sem.at[1], sibling)
    own_patches.wait()

    def share(slab):
        push(
            pin.at[slab, pl.ds(pl.multiple_of(other * half, half), half)],
            pnear.at[slab], near_send.at[slab], near_recv.at[slab], sibling,
        )

    share(z)

    for oz in range(Z):
        for orow in range(R):
            if (oz, orow) != (0, 0):
                src = lax.rem(z + Z - oz, Z) * R + lax.rem(r + R - orow, R)
                landed(ids.at[src], l_recv.at[oz * R + orow])
    for zz in range(Z):
        columns = ids[zz * R + r].astype(f32).T
        id_col[zz * half : (zz + 1) * half, :] = jnp.where(
            c == 0, columns[:half, 0:1], columns[:half, 1:2]
        )

    def embed_rows(base):
        def run(t, carry):
            at = pl.multiple_of(base + t * 8, 8)
            patch_id = jnp.maximum(id_col[pl.ds(at, 8), :].astype(jnp.int32), 0)
            coord_x = (patch_id >> 12).astype(f32)
            coord_y = ((patch_id >> 6) & (GRID - 1)).astype(f32)
            coord_z = (patch_id & (GRID - 1)).astype(f32)
            coord = jnp.where(pick == 0, coord_x, jnp.where(pick == 1, coord_y, coord_z))
            hid[pl.ds(at, 8), :] = sine(coord * frequency + phase)
            return carry

        lax.fori_loop(0, half // 8, run, 0)

    row0 = pl.multiple_of(c * half, half)

    def norm_slab(slab):
        landed(pnear.at[slab], near_recv.at[slab])
        base = pl.multiple_of(slab * half, half)

        def run(t, carry):
            at = pl.multiple_of(t * 16, 16)
            mine = pin[slab, pl.ds(row0 + at, 16), :]
            theirs = pnear[slab, pl.ds(at, 16), :]
            left = jnp.where(c == 0, mine, theirs)
            right = jnp.where(c == 0, theirs, mine)
            embedded = jnp.concatenate([left, right], axis=1)
            hidden = embedded.astype(f32) + hid[pl.ds(base + at, 16), :]
            center = hidden - jnp.mean(hidden, axis=1, keepdims=True)
            spread = jnp.mean(center * center, axis=1, keepdims=True)
            normed = center * lax.rsqrt(spread + 1e-06) * gain[...] + bias[...]
            xs[pl.ds(base + at, 16), :] = normed.astype(bf16)
            return carry

        lax.fori_loop(0, half // 16, run, 0)

    def weight_rows(i, src_row, cc, part=None):
        start = src_row * depth + cc * sub
        if part is None:
            return wfull.at[i, pl.ds(pl.multiple_of(start, sub), sub)]
        start = pl.multiple_of(start + part * (sub // 2), sub // 2)
        return wfull.at[i, pl.ds(start, sub // 2)]

    def weights_on(i):
        for o in NEAR:
            landed(weight_rows(i, r ^ o, c), w_recv.at[i, o])
            step = NEAR[1 - NEAR.index(o)]
            half_block = weight_rows(i, r ^ o, c, NEAR.index(o))
            push(half_block, half_block, d_send.at[i, o - 1], d_recv.at[i, o - 1], device(z, r ^ step, c))
            block = weight_rows(i, r ^ o, c)
            push(block, block, wf_sem.at[0, i, o], wf_sem.at[1, i, o], sibling)

    def weights_far(i):
        far = r ^ NEAR[0] ^ NEAR[1]
        for o in NEAR:
            landed(weight_rows(i, far, c, NEAR.index(o)), d_recv.at[i, o - 1])
        block = weight_rows(i, far, c)
        push(block, block, wf_sem.at[0, i, 3], wf_sem.at[1, i, 3], sibling)

    for zz in range(Z):
        embed_rows(zz * half)
    norm_slab(z)
    weights_on(0)
    for far in range(1, Z):
        for up in (True, False):
            slab = z - far if up else z + far

            @pl.when(z >= far if up else z + far < Z)
            def _():
                landed(pin.at[slab], z_recv.at[0 if up else 1, far])

            if far < Z - 1:
                @pl.when(passes(up, far))
                def _():
                    hop(up, far).start()

            @pl.when(z >= far if up else z + far < Z)
            def _():
                remote(
                    pin.at[slab, pl.ds(pl.multiple_of(other * half, half), half)],
                    pnear.at[slab], near_send.at[slab], near_recv.at[slab], sibling,
                ).start()

        if far == 1:
            columns = ids[...].astype(f32).reshape(Z * R * 8, 128).T
            dead = jnp.where(columns < 0.0, DEAD, 0.0)
            for zz in range(Z):
                for rr in range(R):
                    for cc in range(2):
                        at = (zz * R + rr) * 8 + cc
                        key_bias[cc, rr, zz * half : (zz + 1) * half, :] = dead[:half, at : at + 1]
        if far <= 2:
            weights_on(far)
        if far > 1:
            weights_far(far - 2)
        for up in (True, False):
            slab = z - far if up else z + far

            @pl.when(z >= far if up else z + far < Z)
            def _():
                norm_slab(slab)

    weights_far(2)

    scale = 1.0 / math.sqrt(hd)
    for i in range(3):
        mine = wfull.at[i, pl.ds(pl.multiple_of(r * depth, depth), depth)]

        @pl.when(c == owner)
        def _():
            landed(mine, w_own.at[i])

        @pl.when(c != owner)
        def _():
            landed(mine, w_near.at[i])

        for o in range(1, R):
            landed(weight_rows(i, r ^ o, other), wf_sem.at[1, i, o])
        for j in range(0, R, 2):
            pair = jnp.dot(
                xs[...], wfull[i, :, j * hd : (j + 2) * hd], preferred_element_type=f32
            )
            if i == 0:
                pair = pair * scale
            pair = pair.astype(bf16)
            if i == 0:
                pair = jnp.concatenate(
                    [
                        pair[zz * half + b * STEP : zz * half + (b + 1) * STEP]
                        for b in range(blocks)
                        for zz in range(Z)
                    ],
                    axis=0,
                )
            send[i, j] = pair[:, :hd]
            send[i, j + 1] = pair[:, hd:]
        for o in range(1, R):
            j = lax.rem(r + o, R)
            dst = queries.at[r] if i == 0 else kv.at[i - 1, c, r]
            push(send.at[i, j], dst, a_send.at[i, o], a_recv.at[i, o], device(z, j, c))
        if i == 0:
            queries[r] = send[i, r]
        else:
            kv[i - 1, c, r] = send[i, r]
            push(send.at[i, r], kv.at[i - 1, c, r], f_send.at[i - 1, 0], f_recv.at[i - 1, 0], sibling)
    for o in range(1, R):
        landed(queries.at[lax.rem(r + R - o, R)], a_recv.at[0, o])

    def keys_on(i, o):
        block = kv.at[i, c, lax.rem(r + R - o, R)]
        landed(block, a_recv.at[i + 1, o])
        push(block, block, f_send.at[i, o], f_recv.at[i, o], sibling)

    head = z * R + r
    group = head // Z
    lane0 = pl.multiple_of(lax.rem(head, Z) * hd, hd)
    chunk = Z * STEP
    wide = R * chunk

    def mixed_copy(b, zz):
        return remote(
            mixed.at[b, :, zz],
            mrec.at[b, :, :, pl.ds(lane0, hd)],
            m_send.at[b, zz],
            m_recv.at[lax.rem(head, Z), b],
            device(zz, group, c),
        )

    def attend(b):
        query = queries[:, b * chunk : (b + 1) * chunk, :].reshape(wide, hd)
        best = jnp.full((1, wide), DEAD, f32)
        for oc in range(2):
            for o in range(R):
                cc, rr = lax.rem(c + oc, 2), lax.rem(r + R - o, R)
                if b == 0 and oc == 0 and o > 0:
                    keys_on(0, o)
                if b == 0 and oc == 1:
                    landed(kv.at[0, cc, rr], f_recv.at[0, o])
                score = lax.dot_general(
                    kv[0, cc, rr], query, (((1,), (1,)), ((), ())), preferred_element_type=f32
                )
                score = score + key_bias[cc, rr]
                scores[oc, o] = score
                best = jnp.maximum(best, jnp.max(score, axis=0, keepdims=True))
        totals = jnp.zeros((1, wide), f32)
        accum = jnp.zeros((hd, wide), f32)
        if b == 0:
            for o in range(1, R):
                keys_on(1, o)
        for oc in range(2):
            for o in range(R):
                cc, rr = lax.rem(c + oc, 2), lax.rem(r + R - o, R)
                if b == 0 and oc == 1:
                    landed(kv.at[1, cc, rr], f_recv.at[1, o])
                weight = jnp.exp(scores[oc, o] - best)
                totals = totals + jnp.sum(weight, axis=0, keepdims=True)
                accum = accum + lax.dot_general(
                    kv[1, cc, rr], weight.astype(bf16), (((0,), (0,)), ((), ())),
                    preferred_element_type=f32,
                )
        mixed[b] = (accum / totals).T.astype(bf16).reshape(R, Z, STEP, hd)
        for zz in range(Z):
            here = jnp.logical_and(z == zz, group == r)

            @pl.when(jnp.logical_not(here))
            def _():
                mixed_copy(b, zz).start()

            @pl.when(here)
            def _():
                mrec[b, :, :, pl.ds(lane0, hd)] = mixed[b, :, zz]

    def project(b):
        for k in range(Z):
            @pl.when(r * Z + k != head)
            def _():
                landed(mrec.at[b, :, :, pl.ds(k * hd, hd)], m_recv.at[k, b])

        for cc in range(2):
            part = jnp.dot(mrec[b].reshape(R * STEP, depth), wo[cc], preferred_element_type=f32)
            parts[b, cc] = part.astype(bf16).reshape(R, STEP, cw)
        dst = got.at[r, c, pl.ds(b * STEP, STEP)]
        for o in range(1, R):
            for oc in range(2):
                j, cc = lax.rem(r + o, R), lax.rem(c + oc, 2)
                push(parts.at[b, cc, j], dst, o_send.at[b, o, oc], o_recv.at[b, o, oc], device(z, j, cc))
        push(parts.at[b, other, r], dst, o_send.at[b, 0, 1], o_recv.at[b, 0, 1], sibling)
        pltpu.make_async_copy(parts.at[b, c, r], dst, o_own.at[b]).start()

    attend(0)
    wo_copy.wait()
    landed(wo.at[other], wo_sem.at[1])
    for b in range(1, blocks):
        attend(b)
        project(b - 1)
    project(blocks - 1)

    for b in range(blocks):
        rows = pl.ds(b * STEP, STEP)
        landed(got.at[r, c, rows], o_own.at[b])
        for o in range(R):
            for oc in range(2):
                if (o, oc) != (0, 0):
                    src = got.at[lax.rem(r + R - o, R), lax.rem(c + oc, 2), rows]
                    landed(src, o_recv.at[b, o, oc])

    for copy in sent:
        copy.wait_send()
    for far in range(Z - 1):
        for up in (True, False):
            @pl.when(passes(up, far))
            def _():
                hop(up, far).wait_send()

    for far in range(1, Z):
        for up in (True, False):
            slab = z - far if up else z + far

            @pl.when(z >= far if up else z + far < Z)
            def _():
                remote(
                    pin.at[slab, pl.ds(pl.multiple_of(other * half, half), half)],
                    pnear.at[slab], near_send.at[slab], near_recv.at[slab], sibling,
                ).wait_send()

    @pl.when(c == owner)
    def _():
        for i in range(3):
            for copy in weight_copies(i):
                copy.wait_send()

    for b in range(blocks):
        for zz in range(Z):
            @pl.when(jnp.logical_not(jnp.logical_and(z == zz, group == r)))
            def _():
                mixed_copy(b, zz).wait_send()


def fused(sizes, patches, visible, ln_gain, ln_bias, w_query, w_key, w_value, w_output):
    Z, R = sizes
    rows, cw = patches.shape
    depth = w_query.shape[0]
    width = depth * R
    half = rows // 2
    hd = HEAD_DIM
    plane = R * hd
    count = Z * half
    blocks = half // STEP
    vmem = pl.BlockSpec(memory_space=pltpu.VMEM)
    hbm = pl.BlockSpec(memory_space=pl.ANY)
    bf, f32, dma = jnp.bfloat16, jnp.float32, pltpu.SemaphoreType.DMA
    got = pl.pallas_call(
        functools.partial(mesh_kernel, (Z, R, hd)),
        out_shape=jax.ShapeDtypeStruct((R, 2, half, cw), bf),
        in_specs=[hbm] + [vmem] * 3 + [hbm] * 4,
        out_specs=hbm,
        scratch_shapes=[
            pltpu.VMEM((Z * R, 8, 128), jnp.int32),
            pltpu.VMEM((count, 1), f32),
            pltpu.VMEM((Z, rows, cw), bf),
            pltpu.VMEM((Z, half, cw), bf),
            pltpu.VMEM((count, width), f32),
            pltpu.VMEM((3, width, plane), bf),
            pltpu.VMEM((2, depth, cw), bf),
            pltpu.VMEM((count, width), bf),
            pltpu.VMEM((3, R, count, hd), bf),
            pltpu.VMEM((R, count, hd), bf),
            pltpu.VMEM((2, 2, R, count, hd), bf),
            pltpu.VMEM((2, R, count, 1), f32),
            pltpu.VMEM((2, R, count, R * Z * STEP), f32),
            pltpu.VMEM((blocks, R, Z, STEP, hd), bf),
            pltpu.VMEM((blocks, R, STEP, depth), bf),
            pltpu.VMEM((blocks, 2, R, STEP, cw), bf),
            dma,
            dma((2, Z)),
            dma((2, Z)),
            dma((Z,)),
            dma((Z,)),
            dma((3,)),
            dma((3, R, 2)),
            dma((3, R)),
            dma((3,)),
            dma((3,)),
            dma((2, 3, R)),
            dma((3, 2)),
            dma((3, 2)),
            dma((Z * R,)),
            dma((Z * R,)),
            dma((3, R)),
            dma((3, R)),
            dma((2, R)),
            dma((2, R)),
            dma((blocks, Z)),
            dma((Z, blocks)),
            dma((blocks, R, 2)),
            dma((blocks, R, 2)),
            dma((blocks,)),
        ],
        compiler_params=pltpu.CompilerParams(
            collective_id=0, has_side_effects=True, vmem_limit_bytes=56 * 1024 * 1024
        ),
    )(patches, visible.reshape(1, rows), ln_gain.reshape(1, width), ln_bias.reshape(1, width),
      w_query, w_key, w_value, w_output)
    return jnp.sum(got.astype(f32), axis=0).reshape(rows, cw)


def fits(mesh, patches, w_query):
    Z, R, C = mesh.shape["ctx"], mesh.shape["row"], mesh.shape["col"]
    width = w_query.shape[0]
    half = patches.shape[0] // (Z * R * 2)
    return (
        C == 2
        and R == 4
        and Z == 4
        and Z * R * HEAD_DIM == width
        and (width // C) % (R * HEAD_DIM) == 0
        and width // R == Z * HEAD_DIM
        and half % STEP == 0
        and half <= 128
    )


def solution(mesh):
    placed = (
        P(("ctx", "row"), "col"),
        P(("ctx", "row")),
        P(),
        P(),
        P("row", "col"),
        P("row", "col"),
        P("row", "col"),
        P("row", "col"),
    )

    def run(*args):
        part = body
        if fits(mesh, args[0], args[4]):
            part = functools.partial(fused, (mesh.shape["ctx"], mesh.shape["row"]))
        return jax.shard_map(
            part, mesh=mesh, in_specs=placed, out_specs=P(("ctx", "row"), "col"), check_vma=False
        )(*args)

    return run
```

```python
import functools
import math

import jax
import jax.numpy as jnp
from jax import lax
from jax.experimental import pallas as pl
from jax.experimental.pallas import tpu as pltpu
from jax.sharding import PartitionSpec as P

HEAD_DIM = 128
GRID = 64
MESH = pl.DeviceIdType.MESH
DEAD = -1e30
STEP = 32
ONES = 16
NEAR = (1, 2)


def embed(visible, full_width):
    patch_id = jnp.maximum(visible, 0)
    plane_size = GRID * GRID
    coord_x = (patch_id // plane_size).astype(jnp.float32)
    coord_y = (patch_id // GRID % GRID).astype(jnp.float32)
    coord_z = (patch_id % GRID).astype(jnp.float32)
    channel = jnp.arange(full_width, dtype=jnp.int32)
    axis_pick = channel % 3
    frequency = jnp.exp(-math.log(10000.0) * (channel // 6 * 6).astype(jnp.float32) / full_width)
    offset_phase = 0.5 * math.pi * (channel // 3 % 2).astype(jnp.float32)
    picked = jnp.where(
        axis_pick[None, :] == 0,
        coord_x[:, None],
        jnp.where(axis_pick[None, :] == 1, coord_y[:, None], coord_z[:, None]),
    )
    return jnp.sin(picked * frequency[None, :] + offset_phase[None, :])


def normalize(hidden, ln_gain, ln_bias):
    center = hidden - jnp.mean(hidden, axis=1, keepdims=True)
    spread = jnp.mean(center * center, axis=1, keepdims=True)
    return (center * lax.rsqrt(spread + 1e-06) * ln_gain[None, :] + ln_bias[None, :]).astype(
        jnp.bfloat16
    )


def body(patches, visible, ln_gain, ln_bias, w_query, w_key, w_value, w_output):
    rows_full = lax.all_gather(patches, "col", axis=1, tiled=True)
    local_rows = rows_full.shape[0]
    hidden = rows_full.astype(jnp.float32) + embed(visible, rows_full.shape[1])
    normed = normalize(hidden, ln_gain, ln_bias)
    col_width = w_query.shape[1]
    slab_rows = lax.all_gather(normed, "row", axis=0, tiled=True)
    input_start = lax.axis_index("row") * w_query.shape[0]
    own_inputs = lax.dynamic_slice_in_dim(slab_rows, input_start, w_query.shape[0], 1)
    joined = jnp.concatenate([w_query, w_key, w_value], axis=1)
    summed = lax.psum_scatter(
        jnp.dot(own_inputs, joined, preferred_element_type=jnp.float32),
        "row",
        scatter_dimension=0,
        tiled=True,
    )
    query_f = summed[:, :col_width]
    key_f = summed[:, col_width : 2 * col_width]
    value_f = summed[:, 2 * col_width :]
    head_count = col_width // HEAD_DIM
    query = (
        (query_f * (1.0 / math.sqrt(HEAD_DIM)))
        .astype(jnp.bfloat16)
        .reshape(local_rows, head_count, HEAD_DIM)
    )
    keys = key_f.astype(jnp.bfloat16)
    values = value_f.astype(jnp.bfloat16)
    key_live = (visible >= 0).astype(jnp.bfloat16)
    best = jnp.full((head_count, local_rows), -1e30, jnp.float32)
    key_piece = lax.all_gather(keys, ("ctx", "row"), axis=0, tiled=True)
    value_piece = lax.all_gather(values, ("ctx", "row"), axis=0, tiled=True)
    live_piece = lax.all_gather(key_live, ("ctx", "row"), axis=0, tiled=True)
    count = key_piece.shape[0]
    scores = jnp.einsum(
        "qhd,nhd->hqn",
        query,
        key_piece.reshape(count, head_count, HEAD_DIM),
        preferred_element_type=jnp.float32,
    )
    scores = jnp.where(live_piece[None, None, :] > 0, scores, -1e30)
    new_best = jnp.maximum(best, jnp.max(scores, axis=2))
    weights = jnp.exp(scores - new_best[:, :, None])
    totals = jnp.sum(weights, axis=2)
    accum = jnp.einsum(
        "hqn,nhd->hqd",
        weights.astype(jnp.bfloat16),
        value_piece.reshape(count, head_count, HEAD_DIM),
        preferred_element_type=jnp.float32,
    )
    best, totals, accum = (new_best, totals, accum)
    mixed = (
        (accum / totals[:, :, None])
        .transpose(1, 0, 2)
        .reshape(local_rows, col_width)
        .astype(jnp.bfloat16)
    )
    mixed_full = lax.all_gather(mixed, "col", axis=1, tiled=True)
    return jnp.dot(
        mixed_full,
        lax.all_gather(w_output, "row", axis=0, tiled=True),
        preferred_element_type=jnp.float32,
    )


def sine(x):
    turns = jnp.floor(x * (1.0 / math.pi) + 0.5)
    y = x - turns * 3.140625
    y = y - turns * 9.67502593994140625e-4
    y = y - turns * 1.509957990978376432e-7
    odd = turns - 2.0 * jnp.floor(turns * 0.5)
    y = y * (1.0 - 2.0 * odd)
    y2 = y * y
    tail = y2 * (-1.0 / 39916800.0) + 1.0 / 362880.0
    tail = tail * y2 - 1.0 / 5040.0
    tail = tail * y2 + 1.0 / 120.0
    tail = tail * y2 - 1.0 / 6.0
    return y + y * y2 * tail


def mesh_kernel(
    sizes, patches, vis, gain, bias, w_query, w_key, w_value, w_output, got,
    ids, id_col, pin, pnear, hid, wfull, wo, xs, send, queries, kv, key_bias, values, scores, mixed, mrec, parts,
    p_own, z_send, z_recv, near_send, near_recv, wo_sem, w_send, w_recv, w_near, w_own, wf_sem, d_send, d_recv,
    l_send, l_recv, a_send, a_recv, f_send, f_recv, m_send, m_recv, o_send, o_recv, o_own,
):
    Z, R, hd = sizes
    z, r, c = lax.axis_index("ctx"), lax.axis_index("row"), lax.axis_index("col")
    count, full_width = xs.shape
    half = count // Z
    depth, cw = w_query.shape
    plane = wfull.shape[2]
    other = 1 - c
    blocks = half // STEP
    f32, bf16 = jnp.float32, jnp.bfloat16

    def device(zz, rr, cc):
        return {"ctx": zz, "row": rr, "col": cc}

    def remote(src, dst, ssem, rsem, dev):
        return pltpu.make_async_remote_copy(
            src_ref=src, dst_ref=dst, send_sem=ssem, recv_sem=rsem, device_id=dev, device_id_type=MESH
        )

    sent = []

    def push(src, dst, ssem, rsem, dev):
        copy = remote(src, dst, ssem, rsem, dev)
        copy.start()
        sent.append(copy)

    def landed(ref, sem):
        pltpu.make_async_copy(ref, ref, sem).wait()

    sibling = device(z, r, other)
    barrier = pltpu.get_barrier_semaphore()
    for oz in range(Z):
        for orow in range(R):
            for oc in range(2):
                if (oz, orow, oc) != (0, 0, 0) and (oc == 0 or oz == 0):
                    pl.semaphore_signal(
                        barrier,
                        inc=1,
                        device_id=device(lax.rem(z + oz, Z), lax.rem(r + orow, R), lax.rem(c + oc, 2)),
                        device_id_type=MESH,
                    )
    own_patches = pltpu.make_async_copy(patches, pin.at[z], p_own)
    own_patches.start()
    wo_copy = pltpu.make_async_copy(w_output, wo.at[c], wo_sem.at[2])
    wo_copy.start()
    me = z * R + r
    ids[me] = jnp.zeros((8, 128), jnp.int32)
    ids[me, 0:1, 0:half] = vis[:, 0:half]
    ids[me, 1:2, 0:half] = vis[:, half : 2 * half]
    channel = lax.broadcasted_iota(jnp.int32, (1, full_width), 1)
    sixth = channel // 6
    third = channel // 3
    frequency = jnp.exp(-math.log(10000.0) * (sixth * 6).astype(f32) / full_width)
    phase = 0.5 * math.pi * (third % 2).astype(f32)
    pick = channel - third * 3
    pl.semaphore_wait(barrier, Z * R - 1 + R)

    for oz in range(Z):
        for orow in range(R):
            if (oz, orow) != (0, 0):
                push(
                    ids.at[me], ids.at[me], l_send.at[oz * R + orow], l_recv.at[oz * R + orow],
                    device(lax.rem(z + oz, Z), lax.rem(r + orow, R), c),
                )

    def hop(up, far):
        slab = z - far if up else z + far
        block = pin.at[slab]
        src = patches if far == 0 else block
        way = 0 if up else 1
        return remote(
            src, block, z_send.at[way, far], z_recv.at[way, far + 1], device(z + 1 if up else z - 1, r, c)
        )

    def passes(up, far):
        return jnp.logical_and(z >= far, z < Z - 1) if up else jnp.logical_and(z + far < Z, z > 0)

    for up in (True, False):
        @pl.when(passes(up, 0))
        def _():
            hop(up, 0).start()

    weights = (w_query, w_key, w_value)
    owner = (z * plane) // cw
    col0 = pl.multiple_of(lax.rem(z * plane, cw), plane)
    sub = depth // 2

    own_rows = pl.ds(pl.multiple_of(r * depth, depth), depth)

    def weight_near(i):
        src = weights[i].at[:, pl.ds(col0, plane)]
        return remote(src, wfull.at[i, own_rows], w_send.at[i, 0], w_near.at[i], sibling)

    def weight_local(i):
        src = weights[i].at[:, pl.ds(col0, plane)]
        return pltpu.make_async_copy(src, wfull.at[i, own_rows], w_own.at[i])

    @pl.when(c == owner)
    def _():
        for i in range(3):
            weight_near(i).start()
            weight_local(i).start()

    push(w_output, wo.at[c], wo_sem.at[0], wo_sem.at[1], sibling)
    own_patches.wait()

    def share(slab):
        push(
            pin.at[slab, pl.ds(pl.multiple_of(other * half, half), half)],
            pnear.at[slab], near_send.at[slab], near_recv.at[slab], sibling,
        )

    share(z)

    def weight_rows(i, src_row, cc, part=None):
        start = src_row * depth + cc * sub
        if part is None:
            return wfull.at[i, pl.ds(pl.multiple_of(start, sub), sub)]
        start = pl.multiple_of(start + part * (sub // 2), sub // 2)
        return wfull.at[i, pl.ds(start, sub // 2)]

    for i in range(3):
        @pl.when(c == owner)
        def _():
            landed(wfull.at[i, own_rows], w_own.at[i])

        @pl.when(c != owner)
        def _():
            landed(wfull.at[i, own_rows], w_near.at[i])

        for o in NEAR:
            block = weight_rows(i, r, c)
            push(block, block, w_send.at[i, o], w_recv.at[i, o], device(z, r ^ o, c))

    for oz in range(Z):
        for orow in range(R):
            if (oz, orow) != (0, 0):
                src = lax.rem(z + Z - oz, Z) * R + lax.rem(r + R - orow, R)
                landed(ids.at[src], l_recv.at[oz * R + orow])
    for zz in range(Z):
        columns = ids[zz * R + r].astype(f32).T
        id_col[zz * half : (zz + 1) * half, :] = jnp.where(
            c == 0, columns[:half, 0:1], columns[:half, 1:2]
        )

    def embed_rows(base):
        def run(t, carry):
            at = pl.multiple_of(base + t * 8, 8)
            patch_id = jnp.maximum(id_col[pl.ds(at, 8), :].astype(jnp.int32), 0)
            coord_x = (patch_id >> 12).astype(f32)
            coord_y = ((patch_id >> 6) & (GRID - 1)).astype(f32)
            coord_z = (patch_id & (GRID - 1)).astype(f32)
            coord = jnp.where(pick == 0, coord_x, jnp.where(pick == 1, coord_y, coord_z))
            hid[pl.ds(at, 8), :] = sine(coord * frequency + phase)
            return carry

        lax.fori_loop(0, half // 8, run, 0)

    row0 = pl.multiple_of(c * half, half)

    def norm_slab(slab):
        landed(pnear.at[slab], near_recv.at[slab])
        base = pl.multiple_of(slab * half, half)

        def run(t, carry):
            at = pl.multiple_of(t * 16, 16)
            mine = pin[slab, pl.ds(row0 + at, 16), :]
            theirs = pnear[slab, pl.ds(at, 16), :]
            left = jnp.where(c == 0, mine, theirs)
            right = jnp.where(c == 0, theirs, mine)
            embedded = jnp.concatenate([left, right], axis=1)
            hidden = embedded.astype(f32) + hid[pl.ds(base + at, 16), :]
            center = hidden - jnp.mean(hidden, axis=1, keepdims=True)
            spread = jnp.mean(center * center, axis=1, keepdims=True)
            normed = center * lax.rsqrt(spread + 1e-06) * gain[...] + bias[...]
            xs[pl.ds(base + at, 16), :] = normed.astype(bf16)
            return carry

        lax.fori_loop(0, half // 16, run, 0)

    def weights_on(i):
        for o in NEAR:
            landed(weight_rows(i, r ^ o, c), w_recv.at[i, o])
            step = NEAR[1 - NEAR.index(o)]
            half_block = weight_rows(i, r ^ o, c, NEAR.index(o))
            push(half_block, half_block, d_send.at[i, o - 1], d_recv.at[i, o - 1], device(z, r ^ step, c))
            block = weight_rows(i, r ^ o, c)
            push(block, block, wf_sem.at[0, i, o], wf_sem.at[1, i, o], sibling)

    def weights_far(i):
        far = r ^ NEAR[0] ^ NEAR[1]
        for o in NEAR:
            landed(weight_rows(i, far, c, NEAR.index(o)), d_recv.at[i, o - 1])
        block = weight_rows(i, far, c)
        push(block, block, wf_sem.at[0, i, 3], wf_sem.at[1, i, 3], sibling)

    for zz in range(Z):
        embed_rows(zz * half)
    norm_slab(z)
    weights_on(0)
    for far in range(1, Z):
        for up in (True, False):
            slab = z - far if up else z + far

            @pl.when(z >= far if up else z + far < Z)
            def _():
                landed(pin.at[slab], z_recv.at[0 if up else 1, far])

            if far < Z - 1:
                @pl.when(passes(up, far))
                def _():
                    hop(up, far).start()

            @pl.when(z >= far if up else z + far < Z)
            def _():
                remote(
                    pin.at[slab, pl.ds(pl.multiple_of(other * half, half), half)],
                    pnear.at[slab], near_send.at[slab], near_recv.at[slab], sibling,
                ).start()

        if far == 1:
            columns = ids[...].astype(f32).reshape(Z * R * 8, 128).T
            dead = jnp.where(columns < 0.0, DEAD, 0.0)
            first = lax.broadcasted_iota(jnp.int32, (half, hd), 1) == 0
            for zz in range(Z):
                for rr in range(R):
                    for cc in range(2):
                        at = (zz * R + rr) * 8 + cc
                        key_bias[cc, rr, zz * half : (zz + 1) * half, :] = jnp.where(
                            first, dead[:half, at : at + 1], 0.0
                        ).astype(bf16)
        if far <= 2:
            weights_on(far)
        if far > 1:
            weights_far(far - 2)
        for up in (True, False):
            slab = z - far if up else z + far

            @pl.when(z >= far if up else z + far < Z)
            def _():
                norm_slab(slab)

    weights_far(2)

    scale = math.log2(math.e) / math.sqrt(hd)
    for i in range(3):
        for o in range(1, R):
            landed(weight_rows(i, r ^ o, other), wf_sem.at[1, i, o])
        for j in range(0, R, 2):
            pair = jnp.dot(
                xs[...], wfull[i, :, j * hd : (j + 2) * hd], preferred_element_type=f32
            )
            if i == 0:
                pair = pair * scale
            pair = pair.astype(bf16)
            if i == 0:
                pair = jnp.concatenate(
                    [
                        pair[zz * half + b * STEP : zz * half + (b + 1) * STEP]
                        for b in range(blocks)
                        for zz in range(Z)
                    ],
                    axis=0,
                )
            send[i, j] = pair[:, :hd]
            send[i, j + 1] = pair[:, hd:]
        for o in range(1, R):
            j = lax.rem(r + o, R)
            dst = queries.at[r] if i == 0 else kv.at[i - 1, c, r]
            push(send.at[i, j], dst, a_send.at[i, o], a_recv.at[i, o], device(z, j, c))
        if i == 0:
            queries[r] = send[i, r]
        else:
            kv[i - 1, c, r] = send[i, r]
            push(send.at[i, r], kv.at[i - 1, c, r], f_send.at[i - 1, 0], f_recv.at[i - 1, 0], sibling)
    for o in range(1, R):
        landed(queries.at[lax.rem(r + R - o, R)], a_recv.at[0, o])

    def keys_on(i, o):
        block = kv.at[i, c, lax.rem(r + R - o, R)]
        landed(block, a_recv.at[i + 1, o])
        push(block, block, f_send.at[i, o], f_recv.at[i, o], sibling)

    head = z * R + r
    group = head // Z
    lane0 = pl.multiple_of(lax.rem(head, Z) * hd, hd)
    chunk = Z * STEP
    wide = R * chunk

    def mixed_copy(b, zz):
        return remote(
            mixed.at[b, :, zz],
            mrec.at[b, :, :, pl.ds(lane0, hd)],
            m_send.at[b, zz],
            m_recv.at[lax.rem(head, Z), b],
            device(zz, group, c),
        )

    lane = lax.broadcasted_iota(jnp.int32, (wide, hd), 1)

    def attend(b):
        query = queries[:, b * chunk : (b + 1) * chunk, :].reshape(wide, hd)
        query = jnp.concatenate([query, (lane == 0).astype(bf16)], axis=1)
        best = jnp.full((1, wide), DEAD, f32)
        for oc in range(2):
            for o in range(R):
                cc, rr = lax.rem(c + oc, 2), lax.rem(r + R - o, R)
                if b == 0 and oc == 0 and o > 0:
                    keys_on(0, o)
                if b == 0 and oc == 1:
                    landed(kv.at[0, cc, rr], f_recv.at[0, o])
                keys = jnp.concatenate([kv[0, cc, rr], key_bias[cc, rr]], axis=1)
                score = lax.dot_general(
                    keys, query, (((1,), (1,)), ((), ())), preferred_element_type=f32
                )
                scores[oc, o] = score
                best = jnp.maximum(best, jnp.max(score, axis=0, keepdims=True))
        accum = jnp.zeros((hd + ONES, wide), f32)
        if b == 0:
            for o in range(1, R):
                keys_on(1, o)
        for oc in range(2):
            for o in range(R):
                cc, rr = lax.rem(c + oc, 2), lax.rem(r + R - o, R)
                if b == 0 and oc == 1:
                    landed(kv.at[1, cc, rr], f_recv.at[1, o])
                if b == 0:
                    values[oc, o, :hd] = kv[1, cc, rr].T
                    values[oc, o, hd:] = jnp.ones((ONES, count), bf16)
                weight = jnp.exp2(scores[oc, o] - best).astype(bf16)
                accum = accum + jnp.dot(values[oc, o], weight, preferred_element_type=f32)
        mixed[b] = (accum[:hd] / accum[hd : hd + 1]).T.astype(bf16).reshape(R, Z, STEP, hd)
        for zz in range(Z):
            here = jnp.logical_and(z == zz, group == r)

            @pl.when(jnp.logical_not(here))
            def _():
                mixed_copy(b, zz).start()

            @pl.when(here)
            def _():
                mrec[b, :, :, pl.ds(lane0, hd)] = mixed[b, :, zz]

    def project(b):
        for k in range(Z):
            @pl.when(r * Z + k != head)
            def _():
                landed(mrec.at[b, :, :, pl.ds(k * hd, hd)], m_recv.at[k, b])

        for cc in range(2):
            part = jnp.dot(mrec[b].reshape(R * STEP, depth), wo[cc], preferred_element_type=f32)
            parts[b, cc] = part.astype(bf16).reshape(R, STEP, cw)
        dst = got.at[r, c, pl.ds(b * STEP, STEP)]
        for o in range(1, R):
            for oc in range(2):
                j, cc = lax.rem(r + o, R), lax.rem(c + oc, 2)
                push(parts.at[b, cc, j], dst, o_send.at[b, o, oc], o_recv.at[b, o, oc], device(z, j, cc))
        push(parts.at[b, other, r], dst, o_send.at[b, 0, 1], o_recv.at[b, 0, 1], sibling)
        pltpu.make_async_copy(parts.at[b, c, r], dst, o_own.at[b]).start()

    attend(0)
    wo_copy.wait()
    landed(wo.at[other], wo_sem.at[1])
    for b in range(1, blocks):
        attend(b)
        project(b - 1)
    project(blocks - 1)

    for b in range(blocks):
        rows = pl.ds(b * STEP, STEP)
        landed(got.at[r, c, rows], o_own.at[b])
        for o in range(R):
            for oc in range(2):
                if (o, oc) != (0, 0):
                    src = got.at[lax.rem(r + R - o, R), lax.rem(c + oc, 2), rows]
                    landed(src, o_recv.at[b, o, oc])

    for copy in sent:
        copy.wait_send()
    for far in range(Z - 1):
        for up in (True, False):
            @pl.when(passes(up, far))
            def _():
                hop(up, far).wait_send()

    for far in range(1, Z):
        for up in (True, False):
            slab = z - far if up else z + far

            @pl.when(z >= far if up else z + far < Z)
            def _():
                remote(
                    pin.at[slab, pl.ds(pl.multiple_of(other * half, half), half)],
                    pnear.at[slab], near_send.at[slab], near_recv.at[slab], sibling,
                ).wait_send()

    @pl.when(c == owner)
    def _():
        for i in range(3):
            weight_near(i).wait_send()

    for b in range(blocks):
        for zz in range(Z):
            @pl.when(jnp.logical_not(jnp.logical_and(z == zz, group == r)))
            def _():
                mixed_copy(b, zz).wait_send()


def fused(sizes, patches, visible, ln_gain, ln_bias, w_query, w_key, w_value, w_output):
    Z, R = sizes
    rows, cw = patches.shape
    depth = w_query.shape[0]
    width = depth * R
    half = rows // 2
    hd = HEAD_DIM
    plane = R * hd
    count = Z * half
    blocks = half // STEP
    vmem = pl.BlockSpec(memory_space=pltpu.VMEM)
    hbm = pl.BlockSpec(memory_space=pl.ANY)
    bf, f32, dma = jnp.bfloat16, jnp.float32, pltpu.SemaphoreType.DMA
    got = pl.pallas_call(
        functools.partial(mesh_kernel, (Z, R, hd)),
        out_shape=jax.ShapeDtypeStruct((R, 2, half, cw), bf),
        in_specs=[hbm] + [vmem] * 3 + [hbm] * 4,
        out_specs=hbm,
        scratch_shapes=[
            pltpu.VMEM((Z * R, 8, 128), jnp.int32),
            pltpu.VMEM((count, 1), f32),
            pltpu.VMEM((Z, rows, cw), bf),
            pltpu.VMEM((Z, half, cw), bf),
            pltpu.VMEM((count, width), f32),
            pltpu.VMEM((3, width, plane), bf),
            pltpu.VMEM((2, depth, cw), bf),
            pltpu.VMEM((count, width), bf),
            pltpu.VMEM((3, R, count, hd), bf),
            pltpu.VMEM((R, count, hd), bf),
            pltpu.VMEM((2, 2, R, count, hd), bf),
            pltpu.VMEM((2, R, count, hd), bf),
            pltpu.VMEM((2, R, hd + ONES, count), bf),
            pltpu.VMEM((2, R, count, R * Z * STEP), f32),
            pltpu.VMEM((blocks, R, Z, STEP, hd), bf),
            pltpu.VMEM((blocks, R, STEP, depth), bf),
            pltpu.VMEM((blocks, 2, R, STEP, cw), bf),
            dma,
            dma((2, Z)),
            dma((2, Z)),
            dma((Z,)),
            dma((Z,)),
            dma((3,)),
            dma((3, R)),
            dma((3, R)),
            dma((3,)),
            dma((3,)),
            dma((2, 3, R)),
            dma((3, 2)),
            dma((3, 2)),
            dma((Z * R,)),
            dma((Z * R,)),
            dma((3, R)),
            dma((3, R)),
            dma((2, R)),
            dma((2, R)),
            dma((blocks, Z)),
            dma((Z, blocks)),
            dma((blocks, R, 2)),
            dma((blocks, R, 2)),
            dma((blocks,)),
        ],
        compiler_params=pltpu.CompilerParams(
            collective_id=0, has_side_effects=True, vmem_limit_bytes=56 * 1024 * 1024
        ),
    )(patches, visible.reshape(1, rows), ln_gain.reshape(1, width), ln_bias.reshape(1, width),
      w_query, w_key, w_value, w_output)
    return jnp.sum(got.astype(f32), axis=0).reshape(rows, cw)


def fits(mesh, patches, w_query):
    Z, R, C = mesh.shape["ctx"], mesh.shape["row"], mesh.shape["col"]
    width = w_query.shape[0]
    half = patches.shape[0] // (Z * R * 2)
    return (
        C == 2
        and R == 4
        and Z == 4
        and Z * R * HEAD_DIM == width
        and (width // C) % (R * HEAD_DIM) == 0
        and width // R == Z * HEAD_DIM
        and half % STEP == 0
        and half <= 128
    )


def solution(mesh):
    placed = (
        P(("ctx", "row"), "col"),
        P(("ctx", "row")),
        P(),
        P(),
        P("row", "col"),
        P("row", "col"),
        P("row", "col"),
        P("row", "col"),
    )

    def run(*args):
        part = body
        if fits(mesh, args[0], args[4]):
            part = functools.partial(fused, (mesh.shape["ctx"], mesh.shape["row"]))
        return jax.shard_map(
            part, mesh=mesh, in_specs=placed, out_specs=P(("ctx", "row"), "col"), check_vma=False
        )(*args)

    return run
```

```python
import functools
import math

import jax
import jax.numpy as jnp
from jax import lax
from jax.experimental import pallas as pl
from jax.experimental.pallas import tpu as pltpu
from jax.sharding import PartitionSpec as P

HEAD_DIM = 128
GRID = 64
MESH = pl.DeviceIdType.MESH
DEAD = -1e30
STEP = 32
ONES = 16
NEAR = (1, 2)


def embed(visible, full_width):
    patch_id = jnp.maximum(visible, 0)
    plane_size = GRID * GRID
    coord_x = (patch_id // plane_size).astype(jnp.float32)
    coord_y = (patch_id // GRID % GRID).astype(jnp.float32)
    coord_z = (patch_id % GRID).astype(jnp.float32)
    channel = jnp.arange(full_width, dtype=jnp.int32)
    axis_pick = channel % 3
    frequency = jnp.exp(-math.log(10000.0) * (channel // 6 * 6).astype(jnp.float32) / full_width)
    offset_phase = 0.5 * math.pi * (channel // 3 % 2).astype(jnp.float32)
    picked = jnp.where(
        axis_pick[None, :] == 0,
        coord_x[:, None],
        jnp.where(axis_pick[None, :] == 1, coord_y[:, None], coord_z[:, None]),
    )
    return jnp.sin(picked * frequency[None, :] + offset_phase[None, :])


def normalize(hidden, ln_gain, ln_bias):
    center = hidden - jnp.mean(hidden, axis=1, keepdims=True)
    spread = jnp.mean(center * center, axis=1, keepdims=True)
    return (center * lax.rsqrt(spread + 1e-06) * ln_gain[None, :] + ln_bias[None, :]).astype(
        jnp.bfloat16
    )


def body(patches, visible, ln_gain, ln_bias, w_query, w_key, w_value, w_output):
    rows_full = lax.all_gather(patches, "col", axis=1, tiled=True)
    local_rows = rows_full.shape[0]
    hidden = rows_full.astype(jnp.float32) + embed(visible, rows_full.shape[1])
    normed = normalize(hidden, ln_gain, ln_bias)
    col_width = w_query.shape[1]
    slab_rows = lax.all_gather(normed, "row", axis=0, tiled=True)
    input_start = lax.axis_index("row") * w_query.shape[0]
    own_inputs = lax.dynamic_slice_in_dim(slab_rows, input_start, w_query.shape[0], 1)
    joined = jnp.concatenate([w_query, w_key, w_value], axis=1)
    summed = lax.psum_scatter(
        jnp.dot(own_inputs, joined, preferred_element_type=jnp.float32),
        "row",
        scatter_dimension=0,
        tiled=True,
    )
    query_f = summed[:, :col_width]
    key_f = summed[:, col_width : 2 * col_width]
    value_f = summed[:, 2 * col_width :]
    head_count = col_width // HEAD_DIM
    query = (
        (query_f * (1.0 / math.sqrt(HEAD_DIM)))
        .astype(jnp.bfloat16)
        .reshape(local_rows, head_count, HEAD_DIM)
    )
    keys = key_f.astype(jnp.bfloat16)
    values = value_f.astype(jnp.bfloat16)
    key_live = (visible >= 0).astype(jnp.bfloat16)
    best = jnp.full((head_count, local_rows), -1e30, jnp.float32)
    key_piece = lax.all_gather(keys, ("ctx", "row"), axis=0, tiled=True)
    value_piece = lax.all_gather(values, ("ctx", "row"), axis=0, tiled=True)
    live_piece = lax.all_gather(key_live, ("ctx", "row"), axis=0, tiled=True)
    count = key_piece.shape[0]
    scores = jnp.einsum(
        "qhd,nhd->hqn",
        query,
        key_piece.reshape(count, head_count, HEAD_DIM),
        preferred_element_type=jnp.float32,
    )
    scores = jnp.where(live_piece[None, None, :] > 0, scores, -1e30)
    new_best = jnp.maximum(best, jnp.max(scores, axis=2))
    weights = jnp.exp(scores - new_best[:, :, None])
    totals = jnp.sum(weights, axis=2)
    accum = jnp.einsum(
        "hqn,nhd->hqd",
        weights.astype(jnp.bfloat16),
        value_piece.reshape(count, head_count, HEAD_DIM),
        preferred_element_type=jnp.float32,
    )
    best, totals, accum = (new_best, totals, accum)
    mixed = (
        (accum / totals[:, :, None])
        .transpose(1, 0, 2)
        .reshape(local_rows, col_width)
        .astype(jnp.bfloat16)
    )
    mixed_full = lax.all_gather(mixed, "col", axis=1, tiled=True)
    return jnp.dot(
        mixed_full,
        lax.all_gather(w_output, "row", axis=0, tiled=True),
        preferred_element_type=jnp.float32,
    )


def sine(x):
    turns = jnp.floor(x * (1.0 / math.pi) + 0.5)
    y = x - turns * 3.140625
    y = y - turns * 9.67502593994140625e-4
    y = y - turns * 1.509957990978376432e-7
    odd = turns - 2.0 * jnp.floor(turns * 0.5)
    y = y * (1.0 - 2.0 * odd)
    y2 = y * y
    tail = y2 * (-1.0 / 39916800.0) + 1.0 / 362880.0
    tail = tail * y2 - 1.0 / 5040.0
    tail = tail * y2 + 1.0 / 120.0
    tail = tail * y2 - 1.0 / 6.0
    return y + y * y2 * tail


def mesh_kernel(
    sizes, patches, vis, gain, bias, w_query, w_key, w_value, w_output, got,
    ids, id_col, pin, pnear, hid, wfull, wo, xs, send, queries, kv, key_bias, values, scores, mixed, mrec, parts,
    p_own, z_send, z_recv, near_send, near_recv, wo_sem, w_send, w_recv, w_near, w_own, wf_sem, d_send, d_recv,
    l_send, l_recv, a_send, a_recv, f_send, f_recv, m_send, m_recv, o_send, o_recv, o_own,
):
    Z, R, hd = sizes
    z, r, c = lax.axis_index("ctx"), lax.axis_index("row"), lax.axis_index("col")
    count, full_width = xs.shape
    half = count // Z
    depth, cw = w_query.shape
    plane = wfull.shape[2]
    other = 1 - c
    blocks = half // STEP
    f32, bf16 = jnp.float32, jnp.bfloat16

    def device(zz, rr, cc):
        return {"ctx": zz, "row": rr, "col": cc}

    def remote(src, dst, ssem, rsem, dev):
        return pltpu.make_async_remote_copy(
            src_ref=src, dst_ref=dst, send_sem=ssem, recv_sem=rsem, device_id=dev, device_id_type=MESH
        )

    sent = []

    def push(src, dst, ssem, rsem, dev):
        copy = remote(src, dst, ssem, rsem, dev)
        copy.start()
        sent.append(copy)

    def landed(ref, sem):
        pltpu.make_async_copy(ref, ref, sem).wait()

    sibling = device(z, r, other)
    barrier = pltpu.get_barrier_semaphore()
    for oz in range(Z):
        for orow in range(R):
            for oc in range(2):
                if (oz, orow, oc) != (0, 0, 0) and (oc == 0 or oz == 0):
                    pl.semaphore_signal(
                        barrier,
                        inc=1,
                        device_id=device(lax.rem(z + oz, Z), lax.rem(r + orow, R), lax.rem(c + oc, 2)),
                        device_id_type=MESH,
                    )
    own_patches = pltpu.make_async_copy(patches, pin.at[z], p_own)
    own_patches.start()
    wo_copy = pltpu.make_async_copy(w_output, wo.at[c], wo_sem.at[2])
    wo_copy.start()
    me = z * R + r
    ids[me] = jnp.zeros((8, 128), jnp.int32)
    ids[me, 0:1, 0:half] = vis[:, 0:half]
    ids[me, 1:2, 0:half] = vis[:, half : 2 * half]
    channel = lax.broadcasted_iota(jnp.int32, (1, full_width), 1)
    sixth = channel // 6
    third = channel // 3
    frequency = jnp.exp(-math.log(10000.0) * (sixth * 6).astype(f32) / full_width)
    phase = 0.5 * math.pi * (third % 2).astype(f32)
    pick = channel - third * 3
    pl.semaphore_wait(barrier, Z * R - 1 + R)

    for oz in range(Z):
        for orow in range(R):
            if (oz, orow) != (0, 0):
                push(
                    ids.at[me], ids.at[me], l_send.at[oz * R + orow], l_recv.at[oz * R + orow],
                    device(lax.rem(z + oz, Z), lax.rem(r + orow, R), c),
                )

    def hop(up, far):
        slab = z - far if up else z + far
        block = pin.at[slab]
        src = patches if far == 0 else block
        way = 0 if up else 1
        return remote(
            src, block, z_send.at[way, far], z_recv.at[way, far + 1], device(z + 1 if up else z - 1, r, c)
        )

    def passes(up, far):
        return jnp.logical_and(z >= far, z < Z - 1) if up else jnp.logical_and(z + far < Z, z > 0)

    for up in (True, False):
        @pl.when(passes(up, 0))
        def _():
            hop(up, 0).start()

    weights = (w_query, w_key, w_value)
    owner = (z * plane) // cw
    col0 = pl.multiple_of(lax.rem(z * plane, cw), plane)
    sub = depth // 2

    own_rows = pl.ds(pl.multiple_of(r * depth, depth), depth)

    def weight_copies(i):
        src = weights[i]
        copies = []
        for o in NEAR:
            for cc in range(2):
                copies.append(
                    remote(
                        src.at[pl.ds(cc * sub, sub), pl.ds(col0, plane)],
                        wfull.at[i, pl.ds(pl.multiple_of(r * depth + cc * sub, sub), sub)],
                        w_send.at[i, o, cc],
                        w_recv.at[i, o],
                        device(z, r ^ o, cc),
                    )
                )
        own = wfull.at[i, pl.ds(pl.multiple_of(r * depth, depth), depth)]
        copies.append(
            remote(src.at[:, pl.ds(col0, plane)], own, w_send.at[i, 0, 0], w_near.at[i], sibling)
        )
        return copies

    def weight_local(i):
        own = wfull.at[i, pl.ds(pl.multiple_of(r * depth, depth), depth)]
        return pltpu.make_async_copy(weights[i].at[:, pl.ds(col0, plane)], own, w_own.at[i])

    @pl.when(c == owner)
    def _():
        for i in range(3):
            for copy in weight_copies(i):
                copy.start()
            weight_local(i).start()

    push(w_output, wo.at[c], wo_sem.at[0], wo_sem.at[1], sibling)
    own_patches.wait()

    def share(slab):
        push(
            pin.at[slab, pl.ds(pl.multiple_of(other * half, half), half)],
            pnear.at[slab], near_send.at[slab], near_recv.at[slab], sibling,
        )

    share(z)

    def weight_rows(i, src_row, cc, part=None):
        start = src_row * depth + cc * sub
        if part is None:
            return wfull.at[i, pl.ds(pl.multiple_of(start, sub), sub)]
        start = pl.multiple_of(start + part * (sub // 2), sub // 2)
        return wfull.at[i, pl.ds(start, sub // 2)]

    for oz in range(Z):
        for orow in range(R):
            if (oz, orow) != (0, 0):
                src = lax.rem(z + Z - oz, Z) * R + lax.rem(r + R - orow, R)
                landed(ids.at[src], l_recv.at[oz * R + orow])
    for zz in range(Z):
        columns = ids[zz * R + r].astype(f32).T
        id_col[zz * half : (zz + 1) * half, :] = jnp.where(
            c == 0, columns[:half, 0:1], columns[:half, 1:2]
        )

    def embed_rows(base):
        def run(t, carry):
            at = pl.multiple_of(base + t * 8, 8)
            patch_id = jnp.maximum(id_col[pl.ds(at, 8), :].astype(jnp.int32), 0)
            coord_x = (patch_id >> 12).astype(f32)
            coord_y = ((patch_id >> 6) & (GRID - 1)).astype(f32)
            coord_z = (patch_id & (GRID - 1)).astype(f32)
            coord = jnp.where(pick == 0, coord_x, jnp.where(pick == 1, coord_y, coord_z))
            hid[pl.ds(at, 8), :] = sine(coord * frequency + phase)
            return carry

        lax.fori_loop(0, half // 8, run, 0)

    row0 = pl.multiple_of(c * half, half)

    def norm_slab(slab):
        landed(pnear.at[slab], near_recv.at[slab])
        base = pl.multiple_of(slab * half, half)

        def run(t, carry):
            at = pl.multiple_of(t * 16, 16)
            mine = pin[slab, pl.ds(row0 + at, 16), :]
            theirs = pnear[slab, pl.ds(at, 16), :]
            left = jnp.where(c == 0, mine, theirs)
            right = jnp.where(c == 0, theirs, mine)
            embedded = jnp.concatenate([left, right], axis=1)
            hidden = embedded.astype(f32) + hid[pl.ds(base + at, 16), :]
            center = hidden - jnp.mean(hidden, axis=1, keepdims=True)
            spread = jnp.mean(center * center, axis=1, keepdims=True)
            normed = center * lax.rsqrt(spread + 1e-06) * gain[...] + bias[...]
            xs[pl.ds(base + at, 16), :] = normed.astype(bf16)
            return carry

        lax.fori_loop(0, half // 16, run, 0)

    def weights_on(i):
        for o in NEAR:
            landed(weight_rows(i, r ^ o, c), w_recv.at[i, o])
            step = NEAR[1 - NEAR.index(o)]
            half_block = weight_rows(i, r ^ o, c, NEAR.index(o))
            push(half_block, half_block, d_send.at[i, o - 1], d_recv.at[i, o - 1], device(z, r ^ step, c))
            block = weight_rows(i, r ^ o, c)
            push(block, block, wf_sem.at[0, i, o], wf_sem.at[1, i, o], sibling)

    def weights_far(i):
        far = r ^ NEAR[0] ^ NEAR[1]
        for o in NEAR:
            landed(weight_rows(i, far, c, NEAR.index(o)), d_recv.at[i, o - 1])
        block = weight_rows(i, far, c)
        push(block, block, wf_sem.at[0, i, 3], wf_sem.at[1, i, 3], sibling)

    for zz in range(Z):
        embed_rows(zz * half)
    norm_slab(z)
    for far in range(1, Z):
        for up in (True, False):
            slab = z - far if up else z + far

            @pl.when(z >= far if up else z + far < Z)
            def _():
                landed(pin.at[slab], z_recv.at[0 if up else 1, far])

            if far < Z - 1:
                @pl.when(passes(up, far))
                def _():
                    hop(up, far).start()

            @pl.when(z >= far if up else z + far < Z)
            def _():
                remote(
                    pin.at[slab, pl.ds(pl.multiple_of(other * half, half), half)],
                    pnear.at[slab], near_send.at[slab], near_recv.at[slab], sibling,
                ).start()

        if far == 1:
            columns = ids[...].astype(f32).reshape(Z * R * 8, 128).T
            dead = jnp.where(columns < 0.0, DEAD, 0.0)
            first = lax.broadcasted_iota(jnp.int32, (half, hd), 1) == 0
            for zz in range(Z):
                for rr in range(R):
                    for cc in range(2):
                        at = (zz * R + rr) * 8 + cc
                        key_bias[cc, rr, zz * half : (zz + 1) * half, :] = jnp.where(
                            first, dead[:half, at : at + 1], 0.0
                        ).astype(bf16)
        if far == 2:
            for i in range(3):
                weights_on(i)
            for i in range(2):
                weights_far(i)
        for up in (True, False):
            slab = z - far if up else z + far

            @pl.when(z >= far if up else z + far < Z)
            def _():
                norm_slab(slab)

    weights_far(2)

    scale = math.log2(math.e) / math.sqrt(hd)
    for i in range(3):
        @pl.when(c == owner)
        def _():
            landed(wfull.at[i, own_rows], w_own.at[i])

        @pl.when(c != owner)
        def _():
            landed(wfull.at[i, own_rows], w_near.at[i])

        for o in range(1, R):
            landed(weight_rows(i, r ^ o, other), wf_sem.at[1, i, o])
        for j in range(0, R, 2):
            pair = jnp.dot(
                xs[...], wfull[i, :, j * hd : (j + 2) * hd], preferred_element_type=f32
            )
            if i == 0:
                pair = pair * scale
            pair = pair.astype(bf16)
            if i == 0:
                pair = jnp.concatenate(
                    [
                        pair[zz * half + b * STEP : zz * half + (b + 1) * STEP]
                        for b in range(blocks)
                        for zz in range(Z)
                    ],
                    axis=0,
                )
            send[i, j] = pair[:, :hd]
            send[i, j + 1] = pair[:, hd:]
        for o in range(1, R):
            j = lax.rem(r + o, R)
            dst = queries.at[r] if i == 0 else kv.at[i - 1, c, r]
            push(send.at[i, j], dst, a_send.at[i, o], a_recv.at[i, o], device(z, j, c))
        if i == 0:
            queries[r] = send[i, r]
        else:
            kv[i - 1, c, r] = send[i, r]
            push(send.at[i, r], kv.at[i - 1, c, r], f_send.at[i - 1, 0], f_recv.at[i - 1, 0], sibling)
    for o in range(1, R):
        landed(queries.at[lax.rem(r + R - o, R)], a_recv.at[0, o])

    def keys_on(i, o):
        block = kv.at[i, c, lax.rem(r + R - o, R)]
        landed(block, a_recv.at[i + 1, o])
        push(block, block, f_send.at[i, o], f_recv.at[i, o], sibling)

    head = z * R + r
    group = head // Z
    lane0 = pl.multiple_of(lax.rem(head, Z) * hd, hd)
    chunk = Z * STEP
    wide = R * chunk

    def mixed_copy(b, zz):
        return remote(
            mixed.at[b, :, zz],
            mrec.at[b, :, :, pl.ds(lane0, hd)],
            m_send.at[b, zz],
            m_recv.at[lax.rem(head, Z), b],
            device(zz, group, c),
        )

    lane = lax.broadcasted_iota(jnp.int32, (wide, hd), 1)

    def attend(b):
        query = queries[:, b * chunk : (b + 1) * chunk, :].reshape(wide, hd)
        query = jnp.concatenate([query, (lane == 0).astype(bf16)], axis=1)
        best = jnp.full((1, wide), DEAD, f32)
        for oc in range(2):
            for o in range(R):
                cc, rr = lax.rem(c + oc, 2), lax.rem(r + R - o, R)
                if b == 0 and oc == 0 and o > 0:
                    keys_on(0, o)
                if b == 0 and oc == 1:
                    landed(kv.at[0, cc, rr], f_recv.at[0, o])
                keys = jnp.concatenate([kv[0, cc, rr], key_bias[cc, rr]], axis=1)
                score = lax.dot_general(
                    keys, query, (((1,), (1,)), ((), ())), preferred_element_type=f32
                )
                scores[oc, o] = score
                best = jnp.maximum(best, jnp.max(score, axis=0, keepdims=True))
        accum = jnp.zeros((hd + ONES, wide), f32)
        if b == 0:
            for o in range(1, R):
                keys_on(1, o)
        for oc in range(2):
            for o in range(R):
                cc, rr = lax.rem(c + oc, 2), lax.rem(r + R - o, R)
                if b == 0 and oc == 1:
                    landed(kv.at[1, cc, rr], f_recv.at[1, o])
                if b == 0:
                    values[oc, o, :hd] = kv[1, cc, rr].T
                    values[oc, o, hd:] = jnp.ones((ONES, count), bf16)
                weight = jnp.exp2(scores[oc, o] - best).astype(bf16)
                accum = accum + jnp.dot(values[oc, o], weight, preferred_element_type=f32)
        mixed[b] = (accum[:hd] / accum[hd : hd + 1]).T.astype(bf16).reshape(R, Z, STEP, hd)
        for zz in range(Z):
            here = jnp.logical_and(z == zz, group == r)

            @pl.when(jnp.logical_not(here))
            def _():
                mixed_copy(b, zz).start()

            @pl.when(here)
            def _():
                mrec[b, :, :, pl.ds(lane0, hd)] = mixed[b, :, zz]

    def project(b):
        for k in range(Z):
            @pl.when(r * Z + k != head)
            def _():
                landed(mrec.at[b, :, :, pl.ds(k * hd, hd)], m_recv.at[k, b])

        for cc in range(2):
            part = jnp.dot(mrec[b].reshape(R * STEP, depth), wo[cc], preferred_element_type=f32)
            parts[b, cc] = part.astype(bf16).reshape(R, STEP, cw)
        dst = got.at[r, c, pl.ds(b * STEP, STEP)]
        for o in range(1, R):
            for oc in range(2):
                j, cc = lax.rem(r + o, R), lax.rem(c + oc, 2)
                push(parts.at[b, cc, j], dst, o_send.at[b, o, oc], o_recv.at[b, o, oc], device(z, j, cc))
        push(parts.at[b, other, r], dst, o_send.at[b, 0, 1], o_recv.at[b, 0, 1], sibling)
        pltpu.make_async_copy(parts.at[b, c, r], dst, o_own.at[b]).start()

    attend(0)
    wo_copy.wait()
    landed(wo.at[other], wo_sem.at[1])
    for b in range(1, blocks):
        attend(b)
        project(b - 1)
    project(blocks - 1)

    for b in range(blocks):
        rows = pl.ds(b * STEP, STEP)
        landed(got.at[r, c, rows], o_own.at[b])
        for o in range(R):
            for oc in range(2):
                if (o, oc) != (0, 0):
                    src = got.at[lax.rem(r + R - o, R), lax.rem(c + oc, 2), rows]
                    landed(src, o_recv.at[b, o, oc])

    for copy in sent:
        copy.wait_send()
    for far in range(Z - 1):
        for up in (True, False):
            @pl.when(passes(up, far))
            def _():
                hop(up, far).wait_send()

    for far in range(1, Z):
        for up in (True, False):
            slab = z - far if up else z + far

            @pl.when(z >= far if up else z + far < Z)
            def _():
                remote(
                    pin.at[slab, pl.ds(pl.multiple_of(other * half, half), half)],
                    pnear.at[slab], near_send.at[slab], near_recv.at[slab], sibling,
                ).wait_send()

    @pl.when(c == owner)
    def _():
        for i in range(3):
            for copy in weight_copies(i):
                copy.wait_send()

    for b in range(blocks):
        for zz in range(Z):
            @pl.when(jnp.logical_not(jnp.logical_and(z == zz, group == r)))
            def _():
                mixed_copy(b, zz).wait_send()


def fused(sizes, patches, visible, ln_gain, ln_bias, w_query, w_key, w_value, w_output):
    Z, R = sizes
    rows, cw = patches.shape
    depth = w_query.shape[0]
    width = depth * R
    half = rows // 2
    hd = HEAD_DIM
    plane = R * hd
    count = Z * half
    blocks = half // STEP
    vmem = pl.BlockSpec(memory_space=pltpu.VMEM)
    hbm = pl.BlockSpec(memory_space=pl.ANY)
    bf, f32, dma = jnp.bfloat16, jnp.float32, pltpu.SemaphoreType.DMA
    got = pl.pallas_call(
        functools.partial(mesh_kernel, (Z, R, hd)),
        out_shape=jax.ShapeDtypeStruct((R, 2, half, cw), bf),
        in_specs=[hbm] + [vmem] * 3 + [hbm] * 4,
        out_specs=hbm,
        scratch_shapes=[
            pltpu.VMEM((Z * R, 8, 128), jnp.int32),
            pltpu.VMEM((count, 1), f32),
            pltpu.VMEM((Z, rows, cw), bf),
            pltpu.VMEM((Z, half, cw), bf),
            pltpu.VMEM((count, width), f32),
            pltpu.VMEM((3, width, plane), bf),
            pltpu.VMEM((2, depth, cw), bf),
            pltpu.VMEM((count, width), bf),
            pltpu.VMEM((3, R, count, hd), bf),
            pltpu.VMEM((R, count, hd), bf),
            pltpu.VMEM((2, 2, R, count, hd), bf),
            pltpu.VMEM((2, R, count, hd), bf),
            pltpu.VMEM((2, R, hd + ONES, count), bf),
            pltpu.VMEM((2, R, count, R * Z * STEP), f32),
            pltpu.VMEM((blocks, R, Z, STEP, hd), bf),
            pltpu.VMEM((blocks, R, STEP, depth), bf),
            pltpu.VMEM((blocks, 2, R, STEP, cw), bf),
            dma,
            dma((2, Z)),
            dma((2, Z)),
            dma((Z,)),
            dma((Z,)),
            dma((3,)),
            dma((3, R, 2)),
            dma((3, R)),
            dma((3,)),
            dma((3,)),
            dma((2, 3, R)),
            dma((3, 2)),
            dma((3, 2)),
            dma((Z * R,)),
            dma((Z * R,)),
            dma((3, R)),
            dma((3, R)),
            dma((2, R)),
            dma((2, R)),
            dma((blocks, Z)),
            dma((Z, blocks)),
            dma((blocks, R, 2)),
            dma((blocks, R, 2)),
            dma((blocks,)),
        ],
        compiler_params=pltpu.CompilerParams(
            collective_id=0, has_side_effects=True, vmem_limit_bytes=56 * 1024 * 1024
        ),
    )(patches, visible.reshape(1, rows), ln_gain.reshape(1, width), ln_bias.reshape(1, width),
      w_query, w_key, w_value, w_output)
    return jnp.sum(got.astype(f32), axis=0).reshape(rows, cw)


def fits(mesh, patches, w_query):
    Z, R, C = mesh.shape["ctx"], mesh.shape["row"], mesh.shape["col"]
    width = w_query.shape[0]
    half = patches.shape[0] // (Z * R * 2)
    return (
        C == 2
        and R == 4
        and Z == 4
        and Z * R * HEAD_DIM == width
        and (width // C) % (R * HEAD_DIM) == 0
        and width // R == Z * HEAD_DIM
        and half % STEP == 0
        and half <= 128
    )


def solution(mesh):
    placed = (
        P(("ctx", "row"), "col"),
        P(("ctx", "row")),
        P(),
        P(),
        P("row", "col"),
        P("row", "col"),
        P("row", "col"),
        P("row", "col"),
    )

    def run(*args):
        part = body
        if fits(mesh, args[0], args[4]):
            part = functools.partial(fused, (mesh.shape["ctx"], mesh.shape["row"]))
        return jax.shard_map(
            part, mesh=mesh, in_specs=placed, out_specs=P(("ctx", "row"), "col"), check_vma=False
        )(*args)

    return run
```

```python
import functools
import math

import jax
import jax.numpy as jnp
from jax import lax
from jax.experimental import pallas as pl
from jax.experimental.pallas import tpu as pltpu
from jax.sharding import PartitionSpec as P

HEAD_DIM = 128
GRID = 64
MESH = pl.DeviceIdType.MESH
DEAD = -1e30
STEP = 16
ONES = 16
NEAR = (1, 2)


def embed(visible, full_width):
    patch_id = jnp.maximum(visible, 0)
    plane_size = GRID * GRID
    coord_x = (patch_id // plane_size).astype(jnp.float32)
    coord_y = (patch_id // GRID % GRID).astype(jnp.float32)
    coord_z = (patch_id % GRID).astype(jnp.float32)
    channel = jnp.arange(full_width, dtype=jnp.int32)
    axis_pick = channel % 3
    frequency = jnp.exp(-math.log(10000.0) * (channel // 6 * 6).astype(jnp.float32) / full_width)
    offset_phase = 0.5 * math.pi * (channel // 3 % 2).astype(jnp.float32)
    picked = jnp.where(
        axis_pick[None, :] == 0,
        coord_x[:, None],
        jnp.where(axis_pick[None, :] == 1, coord_y[:, None], coord_z[:, None]),
    )
    return jnp.sin(picked * frequency[None, :] + offset_phase[None, :])


def normalize(hidden, ln_gain, ln_bias):
    center = hidden - jnp.mean(hidden, axis=1, keepdims=True)
    spread = jnp.mean(center * center, axis=1, keepdims=True)
    return (center * lax.rsqrt(spread + 1e-06) * ln_gain[None, :] + ln_bias[None, :]).astype(
        jnp.bfloat16
    )


def body(patches, visible, ln_gain, ln_bias, w_query, w_key, w_value, w_output):
    rows_full = lax.all_gather(patches, "col", axis=1, tiled=True)
    local_rows = rows_full.shape[0]
    hidden = rows_full.astype(jnp.float32) + embed(visible, rows_full.shape[1])
    normed = normalize(hidden, ln_gain, ln_bias)
    col_width = w_query.shape[1]
    slab_rows = lax.all_gather(normed, "row", axis=0, tiled=True)
    input_start = lax.axis_index("row") * w_query.shape[0]
    own_inputs = lax.dynamic_slice_in_dim(slab_rows, input_start, w_query.shape[0], 1)
    joined = jnp.concatenate([w_query, w_key, w_value], axis=1)
    summed = lax.psum_scatter(
        jnp.dot(own_inputs, joined, preferred_element_type=jnp.float32),
        "row",
        scatter_dimension=0,
        tiled=True,
    )
    query_f = summed[:, :col_width]
    key_f = summed[:, col_width : 2 * col_width]
    value_f = summed[:, 2 * col_width :]
    head_count = col_width // HEAD_DIM
    query = (
        (query_f * (1.0 / math.sqrt(HEAD_DIM)))
        .astype(jnp.bfloat16)
        .reshape(local_rows, head_count, HEAD_DIM)
    )
    keys = key_f.astype(jnp.bfloat16)
    values = value_f.astype(jnp.bfloat16)
    key_live = (visible >= 0).astype(jnp.bfloat16)
    best = jnp.full((head_count, local_rows), -1e30, jnp.float32)
    key_piece = lax.all_gather(keys, ("ctx", "row"), axis=0, tiled=True)
    value_piece = lax.all_gather(values, ("ctx", "row"), axis=0, tiled=True)
    live_piece = lax.all_gather(key_live, ("ctx", "row"), axis=0, tiled=True)
    count = key_piece.shape[0]
    scores = jnp.einsum(
        "qhd,nhd->hqn",
        query,
        key_piece.reshape(count, head_count, HEAD_DIM),
        preferred_element_type=jnp.float32,
    )
    scores = jnp.where(live_piece[None, None, :] > 0, scores, -1e30)
    new_best = jnp.maximum(best, jnp.max(scores, axis=2))
    weights = jnp.exp(scores - new_best[:, :, None])
    totals = jnp.sum(weights, axis=2)
    accum = jnp.einsum(
        "hqn,nhd->hqd",
        weights.astype(jnp.bfloat16),
        value_piece.reshape(count, head_count, HEAD_DIM),
        preferred_element_type=jnp.float32,
    )
    best, totals, accum = (new_best, totals, accum)
    mixed = (
        (accum / totals[:, :, None])
        .transpose(1, 0, 2)
        .reshape(local_rows, col_width)
        .astype(jnp.bfloat16)
    )
    mixed_full = lax.all_gather(mixed, "col", axis=1, tiled=True)
    return jnp.dot(
        mixed_full,
        lax.all_gather(w_output, "row", axis=0, tiled=True),
        preferred_element_type=jnp.float32,
    )


def sine(x):
    turns = jnp.floor(x * (1.0 / math.pi) + 0.5)
    y = x - turns * 3.140625
    y = y - turns * 9.67502593994140625e-4
    y = y - turns * 1.509957990978376432e-7
    odd = turns - 2.0 * jnp.floor(turns * 0.5)
    y = y * (1.0 - 2.0 * odd)
    y2 = y * y
    tail = y2 * (-1.0 / 39916800.0) + 1.0 / 362880.0
    tail = tail * y2 - 1.0 / 5040.0
    tail = tail * y2 + 1.0 / 120.0
    tail = tail * y2 - 1.0 / 6.0
    return y + y * y2 * tail


def mesh_kernel(
    sizes, patches, vis, gain, bias, w_query, w_key, w_value, w_output, got,
    ids, id_col, pin, pnear, hid, wfull, wo, xs, send, queries, kv, key_bias, values, scores, mixed, mrec, parts,
    p_own, z_send, z_recv, near_send, near_recv, wo_sem, w_send, w_recv, w_near, w_own, wf_sem, d_send, d_recv,
    l_send, l_recv, a_send, a_recv, f_send, f_recv, m_send, m_recv, o_send, o_recv, o_own,
):
    Z, R, hd = sizes
    z, r, c = lax.axis_index("ctx"), lax.axis_index("row"), lax.axis_index("col")
    count, full_width = xs.shape
    half = count // Z
    depth, cw = w_query.shape
    plane = wfull.shape[2]
    other = 1 - c
    blocks = half // STEP
    f32, bf16 = jnp.float32, jnp.bfloat16

    def device(zz, rr, cc):
        return {"ctx": zz, "row": rr, "col": cc}

    def remote(src, dst, ssem, rsem, dev):
        return pltpu.make_async_remote_copy(
            src_ref=src, dst_ref=dst, send_sem=ssem, recv_sem=rsem, device_id=dev, device_id_type=MESH
        )

    sent = []

    def push(src, dst, ssem, rsem, dev):
        copy = remote(src, dst, ssem, rsem, dev)
        copy.start()
        sent.append(copy)

    def landed(ref, sem):
        pltpu.make_async_copy(ref, ref, sem).wait()

    sibling = device(z, r, other)
    barrier = pltpu.get_barrier_semaphore()
    for oz in range(Z):
        for orow in range(R):
            for oc in range(2):
                if (oz, orow, oc) != (0, 0, 0) and (oc == 0 or oz == 0):
                    pl.semaphore_signal(
                        barrier,
                        inc=1,
                        device_id=device(lax.rem(z + oz, Z), lax.rem(r + orow, R), lax.rem(c + oc, 2)),
                        device_id_type=MESH,
                    )
    own_patches = pltpu.make_async_copy(patches, pin.at[z], p_own)
    own_patches.start()
    wo_copy = pltpu.make_async_copy(w_output, wo.at[c], wo_sem.at[2])
    wo_copy.start()
    me = z * R + r
    ids[me] = jnp.zeros((8, 128), jnp.int32)
    ids[me, 0:1, 0:half] = vis[:, 0:half]
    ids[me, 1:2, 0:half] = vis[:, half : 2 * half]
    channel = lax.broadcasted_iota(jnp.int32, (1, full_width), 1)
    sixth = channel // 6
    third = channel // 3
    frequency = jnp.exp(-math.log(10000.0) * (sixth * 6).astype(f32) / full_width)
    phase = 0.5 * math.pi * (third % 2).astype(f32)
    pick = channel - third * 3
    pl.semaphore_wait(barrier, Z * R - 1 + R)

    for oz in range(Z):
        for orow in range(R):
            if (oz, orow) != (0, 0):
                push(
                    ids.at[me], ids.at[me], l_send.at[oz * R + orow], l_recv.at[oz * R + orow],
                    device(lax.rem(z + oz, Z), lax.rem(r + orow, R), c),
                )

    def hop(up, far):
        slab = z - far if up else z + far
        block = pin.at[slab]
        src = patches if far == 0 else block
        way = 0 if up else 1
        return remote(
            src, block, z_send.at[way, far], z_recv.at[way, far + 1], device(z + 1 if up else z - 1, r, c)
        )

    def passes(up, far):
        return jnp.logical_and(z >= far, z < Z - 1) if up else jnp.logical_and(z + far < Z, z > 0)

    for up in (True, False):
        @pl.when(passes(up, 0))
        def _():
            hop(up, 0).start()

    weights = (w_query, w_key, w_value)
    owner = (z * plane) // cw
    col0 = pl.multiple_of(lax.rem(z * plane, cw), plane)
    sub = depth // 2

    own_rows = pl.ds(pl.multiple_of(r * depth, depth), depth)

    def weight_copies(i):
        src = weights[i]
        copies = []
        for o in NEAR:
            for cc in range(2):
                copies.append(
                    remote(
                        src.at[pl.ds(cc * sub, sub), pl.ds(col0, plane)],
                        wfull.at[i, pl.ds(pl.multiple_of(r * depth + cc * sub, sub), sub)],
                        w_send.at[i, o, cc],
                        w_recv.at[i, o],
                        device(z, r ^ o, cc),
                    )
                )
        own = wfull.at[i, pl.ds(pl.multiple_of(r * depth, depth), depth)]
        copies.append(
            remote(src.at[:, pl.ds(col0, plane)], own, w_send.at[i, 0, 0], w_near.at[i], sibling)
        )
        return copies

    def weight_local(i):
        own = wfull.at[i, pl.ds(pl.multiple_of(r * depth, depth), depth)]
        return pltpu.make_async_copy(weights[i].at[:, pl.ds(col0, plane)], own, w_own.at[i])

    @pl.when(c == owner)
    def _():
        for i in range(3):
            for copy in weight_copies(i):
                copy.start()
            weight_local(i).start()

    push(w_output, wo.at[c], wo_sem.at[0], wo_sem.at[1], sibling)
    own_patches.wait()

    def share(slab):
        push(
            pin.at[slab, pl.ds(pl.multiple_of(other * half, half), half)],
            pnear.at[slab], near_send.at[slab], near_recv.at[slab], sibling,
        )

    share(z)

    def weight_rows(i, src_row, cc, part=None):
        start = src_row * depth + cc * sub
        if part is None:
            return wfull.at[i, pl.ds(pl.multiple_of(start, sub), sub)]
        start = pl.multiple_of(start + part * (sub // 2), sub // 2)
        return wfull.at[i, pl.ds(start, sub // 2)]

    for oz in range(Z):
        for orow in range(R):
            if (oz, orow) != (0, 0):
                src = lax.rem(z + Z - oz, Z) * R + lax.rem(r + R - orow, R)
                landed(ids.at[src], l_recv.at[oz * R + orow])
    for zz in range(Z):
        columns = ids[zz * R + r].astype(f32).T
        id_col[zz * half : (zz + 1) * half, :] = jnp.where(
            c == 0, columns[:half, 0:1], columns[:half, 1:2]
        )

    def embed_rows(base):
        def run(t, carry):
            at = pl.multiple_of(base + t * 8, 8)
            patch_id = jnp.maximum(id_col[pl.ds(at, 8), :].astype(jnp.int32), 0)
            coord_x = (patch_id >> 12).astype(f32)
            coord_y = ((patch_id >> 6) & (GRID - 1)).astype(f32)
            coord_z = (patch_id & (GRID - 1)).astype(f32)
            coord = jnp.where(pick == 0, coord_x, jnp.where(pick == 1, coord_y, coord_z))
            hid[pl.ds(at, 8), :] = sine(coord * frequency + phase)
            return carry

        lax.fori_loop(0, half // 8, run, 0)

    row0 = pl.multiple_of(c * half, half)

    def norm_slab(slab):
        landed(pnear.at[slab], near_recv.at[slab])
        base = pl.multiple_of(slab * half, half)

        def run(t, carry):
            at = pl.multiple_of(t * 16, 16)
            mine = pin[slab, pl.ds(row0 + at, 16), :]
            theirs = pnear[slab, pl.ds(at, 16), :]
            left = jnp.where(c == 0, mine, theirs)
            right = jnp.where(c == 0, theirs, mine)
            embedded = jnp.concatenate([left, right], axis=1)
            hidden = embedded.astype(f32) + hid[pl.ds(base + at, 16), :]
            center = hidden - jnp.mean(hidden, axis=1, keepdims=True)
            spread = jnp.mean(center * center, axis=1, keepdims=True)
            normed = center * lax.rsqrt(spread + 1e-06) * gain[...] + bias[...]
            xs[pl.ds(base + at, 16), :] = normed.astype(bf16)
            return carry

        lax.fori_loop(0, half // 16, run, 0)

    def weights_on(i):
        for o in NEAR:
            landed(weight_rows(i, r ^ o, c), w_recv.at[i, o])
            step = NEAR[1 - NEAR.index(o)]
            half_block = weight_rows(i, r ^ o, c, NEAR.index(o))
            push(half_block, half_block, d_send.at[i, o - 1], d_recv.at[i, o - 1], device(z, r ^ step, c))
            block = weight_rows(i, r ^ o, c)
            push(block, block, wf_sem.at[0, i, o], wf_sem.at[1, i, o], sibling)

    def weights_far(i):
        far = r ^ NEAR[0] ^ NEAR[1]
        for o in NEAR:
            landed(weight_rows(i, far, c, NEAR.index(o)), d_recv.at[i, o - 1])
        block = weight_rows(i, far, c)
        push(block, block, wf_sem.at[0, i, 3], wf_sem.at[1, i, 3], sibling)

    for zz in range(Z):
        embed_rows(zz * half)
    norm_slab(z)
    for far in range(1, Z):
        for up in (True, False):
            slab = z - far if up else z + far

            @pl.when(z >= far if up else z + far < Z)
            def _():
                landed(pin.at[slab], z_recv.at[0 if up else 1, far])

            if far < Z - 1:
                @pl.when(passes(up, far))
                def _():
                    hop(up, far).start()

            @pl.when(z >= far if up else z + far < Z)
            def _():
                remote(
                    pin.at[slab, pl.ds(pl.multiple_of(other * half, half), half)],
                    pnear.at[slab], near_send.at[slab], near_recv.at[slab], sibling,
                ).start()

        if far == 1:
            columns = ids[...].astype(f32).reshape(Z * R * 8, 128).T
            dead = jnp.where(columns < 0.0, DEAD, 0.0)
            first = lax.broadcasted_iota(jnp.int32, (half, hd), 1) == 0
            for zz in range(Z):
                for rr in range(R):
                    for cc in range(2):
                        at = (zz * R + rr) * 8 + cc
                        key_bias[cc, rr, zz * half : (zz + 1) * half, :] = jnp.where(
                            first, dead[:half, at : at + 1], 0.0
                        ).astype(bf16)
        if far == 2:
            for i in range(3):
                weights_on(i)
            for i in range(2):
                weights_far(i)
        for up in (True, False):
            slab = z - far if up else z + far

            @pl.when(z >= far if up else z + far < Z)
            def _():
                norm_slab(slab)

    weights_far(2)

    scale = math.log2(math.e) / math.sqrt(hd)
    for i in range(3):
        @pl.when(c == owner)
        def _():
            landed(wfull.at[i, own_rows], w_own.at[i])

        @pl.when(c != owner)
        def _():
            landed(wfull.at[i, own_rows], w_near.at[i])

        for o in range(1, R):
            landed(weight_rows(i, r ^ o, other), wf_sem.at[1, i, o])
        for j in range(0, R, 2):
            pair = jnp.dot(
                xs[...], wfull[i, :, j * hd : (j + 2) * hd], preferred_element_type=f32
            )
            if i == 0:
                pair = pair * scale
            pair = pair.astype(bf16)
            if i == 0:
                pair = jnp.concatenate(
                    [
                        pair[zz * half + b * STEP : zz * half + (b + 1) * STEP]
                        for b in range(blocks)
                        for zz in range(Z)
                    ],
                    axis=0,
                )
            send[i, j] = pair[:, :hd]
            send[i, j + 1] = pair[:, hd:]
        for o in range(1, R):
            j = lax.rem(r + o, R)
            dst = queries.at[r] if i == 0 else kv.at[i - 1, c, r]
            push(send.at[i, j], dst, a_send.at[i, o], a_recv.at[i, o], device(z, j, c))
        if i == 0:
            queries[r] = send[i, r]
        else:
            kv[i - 1, c, r] = send[i, r]
            push(send.at[i, r], kv.at[i - 1, c, r], f_send.at[i - 1, 0], f_recv.at[i - 1, 0], sibling)
    for o in range(1, R):
        landed(queries.at[lax.rem(r + R - o, R)], a_recv.at[0, o])

    def keys_on(i, o):
        block = kv.at[i, c, lax.rem(r + R - o, R)]
        landed(block, a_recv.at[i + 1, o])
        push(block, block, f_send.at[i, o], f_recv.at[i, o], sibling)

    head = z * R + r
    group = head // Z
    lane0 = pl.multiple_of(lax.rem(head, Z) * hd, hd)
    chunk = Z * STEP
    wide = R * chunk

    def mixed_copy(b, zz):
        return remote(
            mixed.at[b, :, zz],
            mrec.at[b, :, :, pl.ds(lane0, hd)],
            m_send.at[b, zz],
            m_recv.at[lax.rem(head, Z), b],
            device(zz, group, c),
        )

    lane = lax.broadcasted_iota(jnp.int32, (wide, hd), 1)

    def attend(b):
        query = queries[:, b * chunk : (b + 1) * chunk, :].reshape(wide, hd)
        query = jnp.concatenate([query, (lane == 0).astype(bf16)], axis=1)
        best = jnp.full((1, wide), DEAD, f32)
        for oc in range(2):
            for o in range(R):
                cc, rr = lax.rem(c + oc, 2), lax.rem(r + R - o, R)
                if b == 0 and oc == 0 and o > 0:
                    keys_on(0, o)
                if b == 0 and oc == 1:
                    landed(kv.at[0, cc, rr], f_recv.at[0, o])
                keys = jnp.concatenate([kv[0, cc, rr], key_bias[cc, rr]], axis=1)
                score = lax.dot_general(
                    keys, query, (((1,), (1,)), ((), ())), preferred_element_type=f32
                )
                scores[oc, o] = score
                best = jnp.maximum(best, jnp.max(score, axis=0, keepdims=True))
        accum = jnp.zeros((hd + ONES, wide), f32)
        if b == 0:
            for o in range(1, R):
                keys_on(1, o)
        for oc in range(2):
            for o in range(R):
                cc, rr = lax.rem(c + oc, 2), lax.rem(r + R - o, R)
                if b == 0 and oc == 1:
                    landed(kv.at[1, cc, rr], f_recv.at[1, o])
                if b == 0:
                    values[oc, o, :hd] = kv[1, cc, rr].T
                    values[oc, o, hd:] = jnp.ones((ONES, count), bf16)
                weight = jnp.exp2(scores[oc, o] - best).astype(bf16)
                accum = accum + jnp.dot(values[oc, o], weight, preferred_element_type=f32)
        mixed[b] = (accum[:hd] / accum[hd : hd + 1]).T.astype(bf16).reshape(R, Z, STEP, hd)
        for zz in range(Z):
            here = jnp.logical_and(z == zz, group == r)

            @pl.when(jnp.logical_not(here))
            def _():
                mixed_copy(b, zz).start()

            @pl.when(here)
            def _():
                mrec[b, :, :, pl.ds(lane0, hd)] = mixed[b, :, zz]

    def project(b):
        for k in range(Z):
            @pl.when(r * Z + k != head)
            def _():
                landed(mrec.at[b, :, :, pl.ds(k * hd, hd)], m_recv.at[k, b])

        for cc in range(2):
            part = jnp.dot(mrec[b].reshape(R * STEP, depth), wo[cc], preferred_element_type=f32)
            parts[b, cc] = part.astype(bf16).reshape(R, STEP, cw)
        dst = got.at[r, c, pl.ds(b * STEP, STEP)]
        for o in range(1, R):
            for oc in range(2):
                j, cc = lax.rem(r + o, R), lax.rem(c + oc, 2)
                push(parts.at[b, cc, j], dst, o_send.at[b, o, oc], o_recv.at[b, o, oc], device(z, j, cc))
        push(parts.at[b, other, r], dst, o_send.at[b, 0, 1], o_recv.at[b, 0, 1], sibling)
        pltpu.make_async_copy(parts.at[b, c, r], dst, o_own.at[b]).start()

    attend(0)
    wo_copy.wait()
    landed(wo.at[other], wo_sem.at[1])
    for b in range(1, blocks):
        attend(b)
        project(b - 1)
    project(blocks - 1)

    for b in range(blocks):
        rows = pl.ds(b * STEP, STEP)
        landed(got.at[r, c, rows], o_own.at[b])
        for o in range(R):
            for oc in range(2):
                if (o, oc) != (0, 0):
                    src = got.at[lax.rem(r + R - o, R), lax.rem(c + oc, 2), rows]
                    landed(src, o_recv.at[b, o, oc])

    for copy in sent:
        copy.wait_send()
    for far in range(Z - 1):
        for up in (True, False):
            @pl.when(passes(up, far))
            def _():
                hop(up, far).wait_send()

    for far in range(1, Z):
        for up in (True, False):
            slab = z - far if up else z + far

            @pl.when(z >= far if up else z + far < Z)
            def _():
                remote(
                    pin.at[slab, pl.ds(pl.multiple_of(other * half, half), half)],
                    pnear.at[slab], near_send.at[slab], near_recv.at[slab], sibling,
                ).wait_send()

    @pl.when(c == owner)
    def _():
        for i in range(3):
            for copy in weight_copies(i):
                copy.wait_send()

    for b in range(blocks):
        for zz in range(Z):
            @pl.when(jnp.logical_not(jnp.logical_and(z == zz, group == r)))
            def _():
                mixed_copy(b, zz).wait_send()


def fused(sizes, patches, visible, ln_gain, ln_bias, w_query, w_key, w_value, w_output):
    Z, R = sizes
    rows, cw = patches.shape
    depth = w_query.shape[0]
    width = depth * R
    half = rows // 2
    hd = HEAD_DIM
    plane = R * hd
    count = Z * half
    blocks = half // STEP
    vmem = pl.BlockSpec(memory_space=pltpu.VMEM)
    hbm = pl.BlockSpec(memory_space=pl.ANY)
    bf, f32, dma = jnp.bfloat16, jnp.float32, pltpu.SemaphoreType.DMA
    got = pl.pallas_call(
        functools.partial(mesh_kernel, (Z, R, hd)),
        out_shape=jax.ShapeDtypeStruct((R, 2, half, cw), bf),
        in_specs=[hbm] + [vmem] * 3 + [hbm] * 4,
        out_specs=hbm,
        scratch_shapes=[
            pltpu.VMEM((Z * R, 8, 128), jnp.int32),
            pltpu.VMEM((count, 1), f32),
            pltpu.VMEM((Z, rows, cw), bf),
            pltpu.VMEM((Z, half, cw), bf),
            pltpu.VMEM((count, width), f32),
            pltpu.VMEM((3, width, plane), bf),
            pltpu.VMEM((2, depth, cw), bf),
            pltpu.VMEM((count, width), bf),
            pltpu.VMEM((3, R, count, hd), bf),
            pltpu.VMEM((R, count, hd), bf),
            pltpu.VMEM((2, 2, R, count, hd), bf),
            pltpu.VMEM((2, R, count, hd), bf),
            pltpu.VMEM((2, R, hd + ONES, count), bf),
            pltpu.VMEM((2, R, count, R * Z * STEP), f32),
            pltpu.VMEM((blocks, R, Z, STEP, hd), bf),
            pltpu.VMEM((blocks, R, STEP, depth), bf),
            pltpu.VMEM((blocks, 2, R, STEP, cw), bf),
            dma,
            dma((2, Z)),
            dma((2, Z)),
            dma((Z,)),
            dma((Z,)),
            dma((3,)),
            dma((3, R, 2)),
            dma((3, R)),
            dma((3,)),
            dma((3,)),
            dma((2, 3, R)),
            dma((3, 2)),
            dma((3, 2)),
            dma((Z * R,)),
            dma((Z * R,)),
            dma((3, R)),
            dma((3, R)),
            dma((2, R)),
            dma((2, R)),
            dma((blocks, Z)),
            dma((Z, blocks)),
            dma((blocks, R, 2)),
            dma((blocks, R, 2)),
            dma((blocks,)),
        ],
        compiler_params=pltpu.CompilerParams(
            collective_id=0, has_side_effects=True, vmem_limit_bytes=56 * 1024 * 1024
        ),
    )(patches, visible.reshape(1, rows), ln_gain.reshape(1, width), ln_bias.reshape(1, width),
      w_query, w_key, w_value, w_output)
    return jnp.sum(got.astype(f32), axis=0).reshape(rows, cw)


def fits(mesh, patches, w_query):
    Z, R, C = mesh.shape["ctx"], mesh.shape["row"], mesh.shape["col"]
    width = w_query.shape[0]
    half = patches.shape[0] // (Z * R * 2)
    return (
        C == 2
        and R == 4
        and Z == 4
        and Z * R * HEAD_DIM == width
        and (width // C) % (R * HEAD_DIM) == 0
        and width // R == Z * HEAD_DIM
        and half % STEP == 0
        and half <= 128
    )


def solution(mesh):
    placed = (
        P(("ctx", "row"), "col"),
        P(("ctx", "row")),
        P(),
        P(),
        P("row", "col"),
        P("row", "col"),
        P("row", "col"),
        P("row", "col"),
    )

    def run(*args):
        part = body
        if fits(mesh, args[0], args[4]):
            part = functools.partial(fused, (mesh.shape["ctx"], mesh.shape["row"]))
        return jax.shard_map(
            part, mesh=mesh, in_specs=placed, out_specs=P(("ctx", "row"), "col"), check_vma=False
        )(*args)

    return run
```

```python
import functools
import math

import jax
import jax.numpy as jnp
from jax import lax
from jax.experimental import pallas as pl
from jax.experimental.pallas import tpu as pltpu
from jax.sharding import PartitionSpec as P

HEAD_DIM = 128
GRID = 64
MESH = pl.DeviceIdType.MESH
DEAD = -1e30
STEP = 32
ONES = 16
NEAR = (1, 2)


def embed(visible, full_width):
    patch_id = jnp.maximum(visible, 0)
    plane_size = GRID * GRID
    coord_x = (patch_id // plane_size).astype(jnp.float32)
    coord_y = (patch_id // GRID % GRID).astype(jnp.float32)
    coord_z = (patch_id % GRID).astype(jnp.float32)
    channel = jnp.arange(full_width, dtype=jnp.int32)
    axis_pick = channel % 3
    frequency = jnp.exp(-math.log(10000.0) * (channel // 6 * 6).astype(jnp.float32) / full_width)
    offset_phase = 0.5 * math.pi * (channel // 3 % 2).astype(jnp.float32)
    picked = jnp.where(
        axis_pick[None, :] == 0,
        coord_x[:, None],
        jnp.where(axis_pick[None, :] == 1, coord_y[:, None], coord_z[:, None]),
    )
    return jnp.sin(picked * frequency[None, :] + offset_phase[None, :])


def normalize(hidden, ln_gain, ln_bias):
    center = hidden - jnp.mean(hidden, axis=1, keepdims=True)
    spread = jnp.mean(center * center, axis=1, keepdims=True)
    return (center * lax.rsqrt(spread + 1e-06) * ln_gain[None, :] + ln_bias[None, :]).astype(
        jnp.bfloat16
    )


def body(patches, visible, ln_gain, ln_bias, w_query, w_key, w_value, w_output):
    rows_full = lax.all_gather(patches, "col", axis=1, tiled=True)
    local_rows = rows_full.shape[0]
    hidden = rows_full.astype(jnp.float32) + embed(visible, rows_full.shape[1])
    normed = normalize(hidden, ln_gain, ln_bias)
    col_width = w_query.shape[1]
    slab_rows = lax.all_gather(normed, "row", axis=0, tiled=True)
    input_start = lax.axis_index("row") * w_query.shape[0]
    own_inputs = lax.dynamic_slice_in_dim(slab_rows, input_start, w_query.shape[0], 1)
    joined = jnp.concatenate([w_query, w_key, w_value], axis=1)
    summed = lax.psum_scatter(
        jnp.dot(own_inputs, joined, preferred_element_type=jnp.float32),
        "row",
        scatter_dimension=0,
        tiled=True,
    )
    query_f = summed[:, :col_width]
    key_f = summed[:, col_width : 2 * col_width]
    value_f = summed[:, 2 * col_width :]
    head_count = col_width // HEAD_DIM
    query = (
        (query_f * (1.0 / math.sqrt(HEAD_DIM)))
        .astype(jnp.bfloat16)
        .reshape(local_rows, head_count, HEAD_DIM)
    )
    keys = key_f.astype(jnp.bfloat16)
    values = value_f.astype(jnp.bfloat16)
    key_live = (visible >= 0).astype(jnp.bfloat16)
    best = jnp.full((head_count, local_rows), -1e30, jnp.float32)
    key_piece = lax.all_gather(keys, ("ctx", "row"), axis=0, tiled=True)
    value_piece = lax.all_gather(values, ("ctx", "row"), axis=0, tiled=True)
    live_piece = lax.all_gather(key_live, ("ctx", "row"), axis=0, tiled=True)
    count = key_piece.shape[0]
    scores = jnp.einsum(
        "qhd,nhd->hqn",
        query,
        key_piece.reshape(count, head_count, HEAD_DIM),
        preferred_element_type=jnp.float32,
    )
    scores = jnp.where(live_piece[None, None, :] > 0, scores, -1e30)
    new_best = jnp.maximum(best, jnp.max(scores, axis=2))
    weights = jnp.exp(scores - new_best[:, :, None])
    totals = jnp.sum(weights, axis=2)
    accum = jnp.einsum(
        "hqn,nhd->hqd",
        weights.astype(jnp.bfloat16),
        value_piece.reshape(count, head_count, HEAD_DIM),
        preferred_element_type=jnp.float32,
    )
    best, totals, accum = (new_best, totals, accum)
    mixed = (
        (accum / totals[:, :, None])
        .transpose(1, 0, 2)
        .reshape(local_rows, col_width)
        .astype(jnp.bfloat16)
    )
    mixed_full = lax.all_gather(mixed, "col", axis=1, tiled=True)
    return jnp.dot(
        mixed_full,
        lax.all_gather(w_output, "row", axis=0, tiled=True),
        preferred_element_type=jnp.float32,
    )


def sine(x):
    turns = jnp.floor(x * (1.0 / math.pi) + 0.5)
    y = x - turns * 3.140625
    y = y - turns * 9.67502593994140625e-4
    y = y - turns * 1.509957990978376432e-7
    odd = turns - 2.0 * jnp.floor(turns * 0.5)
    y = y * (1.0 - 2.0 * odd)
    y2 = y * y
    tail = y2 * (-1.0 / 39916800.0) + 1.0 / 362880.0
    tail = tail * y2 - 1.0 / 5040.0
    tail = tail * y2 + 1.0 / 120.0
    tail = tail * y2 - 1.0 / 6.0
    return y + y * y2 * tail


def mesh_kernel(
    sizes, patches, vis, gain, bias, w_query, w_key, w_value, w_output, got,
    ids, id_col, pin, pnear, hid, wfull, wo, xs, send, queries, kv, key_bias, values, scores, mixed, mrec, parts,
    p_own, z_send, z_recv, near_send, near_recv, wo_sem, w_send, w_recv, w_near, w_own, wf_sem, d_send, d_recv,
    l_send, l_recv, a_send, a_recv, f_send, f_recv, m_send, m_recv, o_send, o_recv, o_own,
):
    Z, R, hd = sizes
    z, r, c = lax.axis_index("ctx"), lax.axis_index("row"), lax.axis_index("col")
    count, full_width = xs.shape
    half = count // Z
    depth, cw = w_query.shape
    plane = wfull.shape[2]
    other = 1 - c
    blocks = half // STEP
    f32, bf16 = jnp.float32, jnp.bfloat16

    def device(zz, rr, cc):
        return {"ctx": zz, "row": rr, "col": cc}

    def remote(src, dst, ssem, rsem, dev):
        return pltpu.make_async_remote_copy(
            src_ref=src, dst_ref=dst, send_sem=ssem, recv_sem=rsem, device_id=dev, device_id_type=MESH
        )

    sent = []

    def push(src, dst, ssem, rsem, dev):
        copy = remote(src, dst, ssem, rsem, dev)
        copy.start()
        sent.append(copy)

    def landed(ref, sem):
        pltpu.make_async_copy(ref, ref, sem).wait()

    sibling = device(z, r, other)
    barrier = pltpu.get_barrier_semaphore()
    for oz in range(Z):
        for orow in range(R):
            for oc in range(2):
                if (oz, orow, oc) != (0, 0, 0) and (oc == 0 or oz == 0):
                    pl.semaphore_signal(
                        barrier,
                        inc=1,
                        device_id=device(lax.rem(z + oz, Z), lax.rem(r + orow, R), lax.rem(c + oc, 2)),
                        device_id_type=MESH,
                    )
    own_patches = pltpu.make_async_copy(patches, pin.at[z], p_own)
    own_patches.start()
    wo_copy = pltpu.make_async_copy(w_output, wo.at[c], wo_sem.at[2])
    wo_copy.start()
    me = z * R + r
    ids[me] = jnp.zeros((8, 128), jnp.int32)
    ids[me, 0:1, 0:half] = vis[:, 0:half]
    ids[me, 1:2, 0:half] = vis[:, half : 2 * half]
    channel = lax.broadcasted_iota(jnp.int32, (1, full_width), 1)
    sixth = channel // 6
    third = channel // 3
    frequency = jnp.exp(-math.log(10000.0) * (sixth * 6).astype(f32) / full_width)
    phase = 0.5 * math.pi * (third % 2).astype(f32)
    pick = channel - third * 3
    pl.semaphore_wait(barrier, Z * R - 1 + R)

    for oz in range(Z):
        for orow in range(R):
            if (oz, orow) != (0, 0):
                push(
                    ids.at[me], ids.at[me], l_send.at[oz * R + orow], l_recv.at[oz * R + orow],
                    device(lax.rem(z + oz, Z), lax.rem(r + orow, R), c),
                )

    def hop(up, far):
        slab = z - far if up else z + far
        block = pin.at[slab]
        src = patches if far == 0 else block
        way = 0 if up else 1
        return remote(
            src, block, z_send.at[way, far], z_recv.at[way, far + 1], device(z + 1 if up else z - 1, r, c)
        )

    def passes(up, far):
        return jnp.logical_and(z >= far, z < Z - 1) if up else jnp.logical_and(z + far < Z, z > 0)

    for up in (True, False):
        @pl.when(passes(up, 0))
        def _():
            hop(up, 0).start()

    weights = (w_query, w_key, w_value)
    owner = (z * plane) // cw
    col0 = pl.multiple_of(lax.rem(z * plane, cw), plane)
    sub = depth // 2

    own_rows = pl.ds(pl.multiple_of(r * depth, depth), depth)

    def weight_copies(i):
        src = weights[i]
        copies = []
        for o in NEAR:
            for cc in range(2):
                copies.append(
                    remote(
                        src.at[pl.ds(cc * sub, sub), pl.ds(col0, plane)],
                        wfull.at[i, pl.ds(pl.multiple_of(r * depth + cc * sub, sub), sub)],
                        w_send.at[i, o, cc],
                        w_recv.at[i, o],
                        device(z, r ^ o, cc),
                    )
                )
        own = wfull.at[i, pl.ds(pl.multiple_of(r * depth, depth), depth)]
        copies.append(
            remote(src.at[:, pl.ds(col0, plane)], own, w_send.at[i, 0, 0], w_near.at[i], sibling)
        )
        return copies

    def weight_local(i):
        own = wfull.at[i, pl.ds(pl.multiple_of(r * depth, depth), depth)]
        return pltpu.make_async_copy(weights[i].at[:, pl.ds(col0, plane)], own, w_own.at[i])

    @pl.when(c == owner)
    def _():
        for i in range(3):
            for copy in weight_copies(i):
                copy.start()
            weight_local(i).start()

    push(w_output, wo.at[c], wo_sem.at[0], wo_sem.at[1], sibling)
    own_patches.wait()

    def share(slab):
        push(
            pin.at[slab, pl.ds(pl.multiple_of(other * half, half), half)],
            pnear.at[slab], near_send.at[slab], near_recv.at[slab], sibling,
        )

    share(z)

    def weight_rows(i, src_row, cc, part=None):
        start = src_row * depth + cc * sub
        if part is None:
            return wfull.at[i, pl.ds(pl.multiple_of(start, sub), sub)]
        start = pl.multiple_of(start + part * (sub // 2), sub // 2)
        return wfull.at[i, pl.ds(start, sub // 2)]

    for oz in range(Z):
        for orow in range(R):
            if (oz, orow) != (0, 0):
                src = lax.rem(z + Z - oz, Z) * R + lax.rem(r + R - orow, R)
                landed(ids.at[src], l_recv.at[oz * R + orow])
    for zz in range(Z):
        columns = ids[zz * R + r].astype(f32).T
        id_col[zz * half : (zz + 1) * half, :] = jnp.where(
            c == 0, columns[:half, 0:1], columns[:half, 1:2]
        )

    def embed_rows(base):
        def run(t, carry):
            at = pl.multiple_of(base + t * 8, 8)
            patch_id = jnp.maximum(id_col[pl.ds(at, 8), :].astype(jnp.int32), 0)
            coord_x = (patch_id >> 12).astype(f32)
            coord_y = ((patch_id >> 6) & (GRID - 1)).astype(f32)
            coord_z = (patch_id & (GRID - 1)).astype(f32)
            coord = jnp.where(pick == 0, coord_x, jnp.where(pick == 1, coord_y, coord_z))
            hid[pl.ds(at, 8), :] = sine(coord * frequency + phase)
            return carry

        lax.fori_loop(0, half // 8, run, 0)

    row0 = pl.multiple_of(c * half, half)

    def norm_slab(slab):
        landed(pnear.at[slab], near_recv.at[slab])
        base = pl.multiple_of(slab * half, half)

        def run(t, carry):
            at = pl.multiple_of(t * 16, 16)
            mine = pin[slab, pl.ds(row0 + at, 16), :]
            theirs = pnear[slab, pl.ds(at, 16), :]
            left = jnp.where(c == 0, mine, theirs)
            right = jnp.where(c == 0, theirs, mine)
            embedded = jnp.concatenate([left, right], axis=1)
            hidden = embedded.astype(f32) + hid[pl.ds(base + at, 16), :]
            center = hidden - jnp.mean(hidden, axis=1, keepdims=True)
            spread = jnp.mean(center * center, axis=1, keepdims=True)
            normed = center * lax.rsqrt(spread + 1e-06) * gain[...] + bias[...]
            xs[pl.ds(base + at, 16), :] = normed.astype(bf16)
            return carry

        lax.fori_loop(0, half // 16, run, 0)

    def weights_on(i):
        for o in NEAR:
            landed(weight_rows(i, r ^ o, c), w_recv.at[i, o])
            step = NEAR[1 - NEAR.index(o)]
            half_block = weight_rows(i, r ^ o, c, NEAR.index(o))
            push(half_block, half_block, d_send.at[i, o - 1], d_recv.at[i, o - 1], device(z, r ^ step, c))
            block = weight_rows(i, r ^ o, c)
            push(block, block, wf_sem.at[0, i, o], wf_sem.at[1, i, o], sibling)

    def weights_far(i):
        far = r ^ NEAR[0] ^ NEAR[1]
        for o in NEAR:
            landed(weight_rows(i, far, c, NEAR.index(o)), d_recv.at[i, o - 1])
        block = weight_rows(i, far, c)
        push(block, block, wf_sem.at[0, i, 3], wf_sem.at[1, i, 3], sibling)

    for zz in range(Z):
        embed_rows(zz * half)
    norm_slab(z)
    for far in range(1, Z):
        for up in (True, False):
            slab = z - far if up else z + far

            @pl.when(z >= far if up else z + far < Z)
            def _():
                landed(pin.at[slab], z_recv.at[0 if up else 1, far])

            if far < Z - 1:
                @pl.when(passes(up, far))
                def _():
                    hop(up, far).start()

            @pl.when(z >= far if up else z + far < Z)
            def _():
                remote(
                    pin.at[slab, pl.ds(pl.multiple_of(other * half, half), half)],
                    pnear.at[slab], near_send.at[slab], near_recv.at[slab], sibling,
                ).start()

        if far == 1:
            columns = ids[...].astype(f32).reshape(Z * R * 8, 128).T
            dead = jnp.where(columns < 0.0, DEAD, 0.0)
            first = lax.broadcasted_iota(jnp.int32, (half, hd), 1) == 0
            for zz in range(Z):
                for rr in range(R):
                    for cc in range(2):
                        at = (zz * R + rr) * 8 + cc
                        key_bias[cc, rr, zz * half : (zz + 1) * half, :] = jnp.where(
                            first, dead[:half, at : at + 1], 0.0
                        ).astype(bf16)
        if far == 2:
            for i in range(3):
                weights_on(i)
            for i in range(2):
                weights_far(i)
        for up in (True, False):
            slab = z - far if up else z + far

            @pl.when(z >= far if up else z + far < Z)
            def _():
                norm_slab(slab)

    weights_far(2)

    scale = math.log2(math.e) / math.sqrt(hd)
    for i in range(3):
        @pl.when(c == owner)
        def _():
            landed(wfull.at[i, own_rows], w_own.at[i])

        @pl.when(c != owner)
        def _():
            landed(wfull.at[i, own_rows], w_near.at[i])

        for o in range(1, R):
            landed(weight_rows(i, r ^ o, other), wf_sem.at[1, i, o])
        for j in range(0, R, 2):
            pair = jnp.dot(
                xs[...], wfull[i, :, j * hd : (j + 2) * hd], preferred_element_type=f32
            )
            if i == 0:
                pair = pair * scale
            pair = pair.astype(bf16)
            if i == 0:
                pair = jnp.concatenate(
                    [
                        pair[zz * half + b * STEP : zz * half + (b + 1) * STEP]
                        for b in range(blocks)
                        for zz in range(Z)
                    ],
                    axis=0,
                )
            send[i, j] = pair[:, :hd]
            send[i, j + 1] = pair[:, hd:]
        for o in range(1, R):
            j = lax.rem(r + o, R)
            dst = queries.at[r] if i == 0 else kv.at[i - 1, c, r]
            push(send.at[i, j], dst, a_send.at[i, o], a_recv.at[i, o], device(z, j, c))
        if i == 0:
            queries[r] = send[i, r]
        else:
            kv[i - 1, c, r] = send[i, r]
            push(send.at[i, r], kv.at[i - 1, c, r], f_send.at[i - 1, 0], f_recv.at[i - 1, 0], sibling)
    for o in range(1, R):
        landed(queries.at[lax.rem(r + R - o, R)], a_recv.at[0, o])

    def keys_on(i, o):
        block = kv.at[i, c, lax.rem(r + R - o, R)]
        landed(block, a_recv.at[i + 1, o])
        push(block, block, f_send.at[i, o], f_recv.at[i, o], sibling)

    head = z * R + r
    group = head // Z
    lane0 = pl.multiple_of(lax.rem(head, Z) * hd, hd)
    chunk = Z * STEP
    wide = R * chunk

    def mixed_copy(b, zz):
        return remote(
            mixed.at[b, :, zz],
            mrec.at[b, :, :, pl.ds(lane0, hd)],
            m_send.at[b, zz],
            m_recv.at[lax.rem(head, Z), b],
            device(zz, group, c),
        )

    lane = lax.broadcasted_iota(jnp.int32, (wide, hd), 1)

    def attend(b):
        query = queries[:, b * chunk : (b + 1) * chunk, :].reshape(wide, hd)
        query = jnp.concatenate([query, (lane == 0).astype(bf16)], axis=1)
        best = jnp.full((1, wide), DEAD, f32)
        for oc in range(2):
            for o in range(R):
                cc, rr = lax.rem(c + oc, 2), lax.rem(r + R - o, R)
                if b == 0 and oc == 0 and o > 0:
                    keys_on(0, o)
                if b == 0 and oc == 1:
                    landed(kv.at[0, cc, rr], f_recv.at[0, o])
                keys = jnp.concatenate([kv[0, cc, rr], key_bias[cc, rr]], axis=1)
                score = lax.dot_general(
                    keys, query, (((1,), (1,)), ((), ())), preferred_element_type=f32
                )
                scores[oc, o] = score
                best = jnp.maximum(best, jnp.max(score, axis=0, keepdims=True))
        if b > 0:
            project(b - 1)
        accum = jnp.zeros((hd + ONES, wide), f32)
        if b == 0:
            for o in range(1, R):
                keys_on(1, o)
        for oc in range(2):
            for o in range(R):
                cc, rr = lax.rem(c + oc, 2), lax.rem(r + R - o, R)
                if b == 0 and oc == 1:
                    landed(kv.at[1, cc, rr], f_recv.at[1, o])
                if b == 0:
                    values[oc, o, :hd] = kv[1, cc, rr].T
                    values[oc, o, hd:] = jnp.ones((ONES, count), bf16)
                weight = jnp.exp2(scores[oc, o] - best).astype(bf16)
                accum = accum + jnp.dot(values[oc, o], weight, preferred_element_type=f32)
        mixed[b] = (accum[:hd] / accum[hd : hd + 1]).T.astype(bf16).reshape(R, Z, STEP, hd)
        for zz in range(Z):
            here = jnp.logical_and(z == zz, group == r)

            @pl.when(jnp.logical_not(here))
            def _():
                mixed_copy(b, zz).start()

            @pl.when(here)
            def _():
                mrec[b, :, :, pl.ds(lane0, hd)] = mixed[b, :, zz]

    def project(b):
        for k in range(Z):
            @pl.when(r * Z + k != head)
            def _():
                landed(mrec.at[b, :, :, pl.ds(k * hd, hd)], m_recv.at[k, b])

        for cc in range(2):
            part = jnp.dot(mrec[b].reshape(R * STEP, depth), wo[cc], preferred_element_type=f32)
            parts[b, cc] = part.astype(bf16).reshape(R, STEP, cw)
        dst = got.at[r, c, pl.ds(b * STEP, STEP)]
        for o in range(1, R):
            for oc in range(2):
                j, cc = lax.rem(r + o, R), lax.rem(c + oc, 2)
                push(parts.at[b, cc, j], dst, o_send.at[b, o, oc], o_recv.at[b, o, oc], device(z, j, cc))
        push(parts.at[b, other, r], dst, o_send.at[b, 0, 1], o_recv.at[b, 0, 1], sibling)
        pltpu.make_async_copy(parts.at[b, c, r], dst, o_own.at[b]).start()

    attend(0)
    wo_copy.wait()
    landed(wo.at[other], wo_sem.at[1])
    for b in range(1, blocks):
        attend(b)
    project(blocks - 1)

    for b in range(blocks):
        rows = pl.ds(b * STEP, STEP)
        landed(got.at[r, c, rows], o_own.at[b])
        for o in range(R):
            for oc in range(2):
                if (o, oc) != (0, 0):
                    src = got.at[lax.rem(r + R - o, R), lax.rem(c + oc, 2), rows]
                    landed(src, o_recv.at[b, o, oc])

    for copy in sent:
        copy.wait_send()
    for far in range(Z - 1):
        for up in (True, False):
            @pl.when(passes(up, far))
            def _():
                hop(up, far).wait_send()

    for far in range(1, Z):
        for up in (True, False):
            slab = z - far if up else z + far

            @pl.when(z >= far if up else z + far < Z)
            def _():
                remote(
                    pin.at[slab, pl.ds(pl.multiple_of(other * half, half), half)],
                    pnear.at[slab], near_send.at[slab], near_recv.at[slab], sibling,
                ).wait_send()

    @pl.when(c == owner)
    def _():
        for i in range(3):
            for copy in weight_copies(i):
                copy.wait_send()

    for b in range(blocks):
        for zz in range(Z):
            @pl.when(jnp.logical_not(jnp.logical_and(z == zz, group == r)))
            def _():
                mixed_copy(b, zz).wait_send()


def fused(sizes, patches, visible, ln_gain, ln_bias, w_query, w_key, w_value, w_output):
    Z, R = sizes
    rows, cw = patches.shape
    depth = w_query.shape[0]
    width = depth * R
    half = rows // 2
    hd = HEAD_DIM
    plane = R * hd
    count = Z * half
    blocks = half // STEP
    vmem = pl.BlockSpec(memory_space=pltpu.VMEM)
    hbm = pl.BlockSpec(memory_space=pl.ANY)
    bf, f32, dma = jnp.bfloat16, jnp.float32, pltpu.SemaphoreType.DMA
    got = pl.pallas_call(
        functools.partial(mesh_kernel, (Z, R, hd)),
        out_shape=jax.ShapeDtypeStruct((R, 2, half, cw), bf),
        in_specs=[hbm] + [vmem] * 3 + [hbm] * 4,
        out_specs=hbm,
        scratch_shapes=[
            pltpu.VMEM((Z * R, 8, 128), jnp.int32),
            pltpu.VMEM((count, 1), f32),
            pltpu.VMEM((Z, rows, cw), bf),
            pltpu.VMEM((Z, half, cw), bf),
            pltpu.VMEM((count, width), f32),
            pltpu.VMEM((3, width, plane), bf),
            pltpu.VMEM((2, depth, cw), bf),
            pltpu.VMEM((count, width), bf),
            pltpu.VMEM((3, R, count, hd), bf),
            pltpu.VMEM((R, count, hd), bf),
            pltpu.VMEM((2, 2, R, count, hd), bf),
            pltpu.VMEM((2, R, count, hd), bf),
            pltpu.VMEM((2, R, hd + ONES, count), bf),
            pltpu.VMEM((2, R, count, R * Z * STEP), f32),
            pltpu.VMEM((blocks, R, Z, STEP, hd), bf),
            pltpu.VMEM((blocks, R, STEP, depth), bf),
            pltpu.VMEM((blocks, 2, R, STEP, cw), bf),
            dma,
            dma((2, Z)),
            dma((2, Z)),
            dma((Z,)),
            dma((Z,)),
            dma((3,)),
            dma((3, R, 2)),
            dma((3, R)),
            dma((3,)),
            dma((3,)),
            dma((2, 3, R)),
            dma((3, 2)),
            dma((3, 2)),
            dma((Z * R,)),
            dma((Z * R,)),
            dma((3, R)),
            dma((3, R)),
            dma((2, R)),
            dma((2, R)),
            dma((blocks, Z)),
            dma((Z, blocks)),
            dma((blocks, R, 2)),
            dma((blocks, R, 2)),
            dma((blocks,)),
        ],
        compiler_params=pltpu.CompilerParams(
            collective_id=0, has_side_effects=True, vmem_limit_bytes=56 * 1024 * 1024
        ),
    )(patches, visible.reshape(1, rows), ln_gain.reshape(1, width), ln_bias.reshape(1, width),
      w_query, w_key, w_value, w_output)
    return jnp.sum(got.astype(f32), axis=0).reshape(rows, cw)


def fits(mesh, patches, w_query):
    Z, R, C = mesh.shape["ctx"], mesh.shape["row"], mesh.shape["col"]
    width = w_query.shape[0]
    half = patches.shape[0] // (Z * R * 2)
    return (
        C == 2
        and R == 4
        and Z == 4
        and Z * R * HEAD_DIM == width
        and (width // C) % (R * HEAD_DIM) == 0
        and width // R == Z * HEAD_DIM
        and half % STEP == 0
        and half <= 128
    )


def solution(mesh):
    placed = (
        P(("ctx", "row"), "col"),
        P(("ctx", "row")),
        P(),
        P(),
        P("row", "col"),
        P("row", "col"),
        P("row", "col"),
        P("row", "col"),
    )

    def run(*args):
        part = body
        if fits(mesh, args[0], args[4]):
            part = functools.partial(fused, (mesh.shape["ctx"], mesh.shape["row"]))
        return jax.shard_map(
            part, mesh=mesh, in_specs=placed, out_specs=P(("ctx", "row"), "col"), check_vma=False
        )(*args)

    return run
```
